32 devices in a mesh: ctx: 8 (over y, x, core), fsdp: 4 (over z).
Axes of the slice: x: 2, y: 2, z: 4, core: 2. Of those that a mesh axis runs over, the one named last changes fastest.
Arguments:
- queries: bfloat16 [2048, 512], P('ctx', 'fsdp'), may hold values from -6 to 6
- keys: bfloat16 [2048, 128], P('ctx'), may hold values from -6 to 6
- values: bfloat16 [2048, 128], P('ctx'), may hold values from -6 to 6
- out_grad: bfloat16 [2048, 512], P('ctx', 'fsdp'), may hold values from -6 to 6
- block_ids: int32 [16], replicated, may hold values from 0 to 15, as said below
- block_mask: int32 [16, 16], replicated, may hold values from 0 to 1, as said below
Outputs:
- query_grad: float32 [2048, 512], P('ctx', 'fsdp')
- key_grad: float32 [2048, 128], P('ctx', 'fsdp')
- value_grad: float32 [2048, 128], P('ctx', 'fsdp')
The draws below stay inside these ranges and needn't reach their ends.
Inputs may be any that keep to these rules, and one draw needn't show every extreme that they name: `block_ids`: A permutation of the 16 sequence blocks; the two entries 2c and 2c + 1, the blocks of the rows of ctx device c, sum to 15. block_mask[i, j] is 1 for j = i and 0 for j > i; below the diagonal it is 0 or 1.
All inputs are finite; a program needn't handle non-finite values.
Results may differ from the reference program's by a relative error of at most 0.025.
Values may be sent and summed in bfloat16 or wider, within the bound.
No kernel may reach another device: no remote copies, remote signals or barrier semaphores. Data moves between devices by JAX's collectives and lax.ppermute only.
A program may use at most 64 MiB of HBM per device.

```python
import jax
import jax.numpy as jnp
from jax import lax

HEAD_DIM = 128
GROUP = 4
QHEADS = 4
KVHEADS = 1
SEQ = 2048
BLOCK = 128
NBLOCKS = 16


def draw_queries(key, part):
    base_draw = jax.random.truncated_normal(jax.random.fold_in(key, 1), -6.0, 6.0, (SEQ, QHEADS * HEAD_DIM), jnp.float32)
    return base_draw.astype(jnp.bfloat16)


def draw_keys(key, part):
    base_draw = jax.random.truncated_normal(jax.random.fold_in(key, 2), -6.0, 6.0, (SEQ, KVHEADS * HEAD_DIM), jnp.float32)
    return base_draw.astype(jnp.bfloat16)


def draw_block_ids(key, part):
    pair_order = jax.random.permutation(jax.random.fold_in(key, 3), NBLOCKS // 2).astype(jnp.int32)
    flip_bits = jax.random.randint(jax.random.fold_in(key, 4), (NBLOCKS // 2,), 0, 2)
    first_block = jnp.where(flip_bits == 1, pair_order, NBLOCKS - 1 - pair_order)
    second_block = NBLOCKS - 1 - first_block
    return jnp.stack([first_block, second_block], axis=1).reshape(NBLOCKS).astype(jnp.int32)


def draw_block_mask(key, part):
    coin_flips = jax.random.randint(jax.random.fold_in(key, 5), (NBLOCKS, NBLOCKS), 0, 2)
    row_index = jnp.arange(NBLOCKS)[:, None]
    col_index = jnp.arange(NBLOCKS)[None, :]
    return jnp.where(col_index < row_index, coin_flips, jnp.where(col_index == row_index, 1, 0)).astype(jnp.int32)


def shard_levels(rng, extent, cuts, low, high):
    gain = 1.0
    for dim, shards_of in cuts:
        heights = jax.random.uniform(jax.random.fold_in(jax.random.fold_in(rng, 6), dim), (shards_of,), jnp.float32, low / len(cuts), high / len(cuts))
        gain = gain * jnp.repeat(jnp.exp(heights), extent[dim] // shards_of).reshape((-1,) + (1,) * (len(extent) - 1 - dim))
    return gain


def centred(own_key, shape, spread, most, pieces=(), kind=jnp.bfloat16):
    values = spread * jax.random.normal(own_key, shape, jnp.float32)
    if pieces:
        values = values * shard_levels(own_key, shape, pieces, -0.22, 0.18)
    return jnp.clip(values, -most, most).astype(kind)


def setup_inputs(seed: int = 0) -> dict:
    key_list = jax.random.split(jax.random.key(seed), 7)
    return {
        "queries": draw_queries(jax.random.fold_in(key_list[6], 71), 0),
        "keys": draw_keys(jax.random.fold_in(key_list[6], 71), 0),
        "values": centred(key_list[2], (SEQ, KVHEADS * HEAD_DIM), 1.0, 6.0, ((0, 8),)),
        "out_grad": centred(key_list[3], (SEQ, QHEADS * HEAD_DIM), 1.0, 6.0, ((0, 8), (1, 4))),
        "block_ids": draw_block_ids(jax.random.fold_in(key_list[6], 71), 0),
        "block_mask": draw_block_mask(jax.random.fold_in(key_list[6], 71), 0),
    }


def reference(queries, keys, values, out_grad, block_ids, block_mask):
    score_scale = HEAD_DIM ** -0.5
    row_ids = jnp.arange(SEQ, dtype=jnp.int32)
    seq_block = block_ids[row_ids // BLOCK]
    position = seq_block * BLOCK + row_ids % BLOCK
    allowed = (block_mask[seq_block[:, None], seq_block[None, :]] == 1) & (position[:, None] >= position[None, :])

    def one_head(head_index):
        group_head = head_index // GROUP
        q_rows = lax.dynamic_slice_in_dim(queries, head_index * HEAD_DIM, HEAD_DIM, 1)
        g_rows = lax.dynamic_slice_in_dim(out_grad, head_index * HEAD_DIM, HEAD_DIM, 1)
        k_rows = lax.dynamic_slice_in_dim(keys, group_head * HEAD_DIM, HEAD_DIM, 1)
        v_rows = lax.dynamic_slice_in_dim(values, group_head * HEAD_DIM, HEAD_DIM, 1)
        scores = jnp.dot(q_rows, k_rows.T, preferred_element_type=jnp.float32) * score_scale
        row_top = jnp.max(jnp.where(allowed, scores, -jnp.inf), axis=1, keepdims=True)
        row_total = jnp.sum(jnp.where(allowed, jnp.exp(scores - row_top), 0.0), axis=1, keepdims=True)
        log_total = row_top + jnp.log(row_total)
        soft_weights = jnp.where(allowed, jnp.exp(scores - log_total), 0.0)
        output = jnp.dot(soft_weights, v_rows.astype(jnp.float32), precision=lax.Precision.HIGHEST)
        row_delta = jnp.sum(g_rows.astype(jnp.float32) * output, axis=1, keepdims=True)
        grad_weights = jnp.dot(g_rows, v_rows.T, preferred_element_type=jnp.float32)
        grad_scores = (soft_weights * (grad_weights - row_delta)).astype(jnp.bfloat16)
        query_term = jnp.dot(grad_scores, k_rows, preferred_element_type=jnp.float32) * score_scale
        key_term = jnp.dot(grad_scores.T, q_rows, preferred_element_type=jnp.float32) * score_scale
        value_term = jnp.dot(soft_weights.astype(jnp.bfloat16).T, g_rows, preferred_element_type=jnp.float32)
        return query_term, key_term, value_term

    query_all, key_all, value_all = lax.map(one_head, jnp.arange(QHEADS, dtype=jnp.int32))
    query_grad = jnp.transpose(query_all, (1, 0, 2)).reshape(SEQ, QHEADS * HEAD_DIM)
    key_sum = key_all.reshape(KVHEADS, GROUP, SEQ, HEAD_DIM).sum(axis=1)
    value_sum = value_all.reshape(KVHEADS, GROUP, SEQ, HEAD_DIM).sum(axis=1)
    key_grad = jnp.transpose(key_sum, (1, 0, 2)).reshape(SEQ, KVHEADS * HEAD_DIM)
    value_grad = jnp.transpose(value_sum, (1, 0, 2)).reshape(SEQ, KVHEADS * HEAD_DIM)
    return (query_grad, key_grad, value_grad)
```

```python
import functools
import math

import jax
import jax.numpy as jnp
from jax import lax
from jax.experimental import pallas as pl
from jax.experimental.pallas import tpu as pltpu
from jax.sharding import PartitionSpec as P

GROUP = 4
SHARE = 4
MASKED = -1e30
FLOOR = -1e20
VMEM_LIMIT = 48 * 1024 * 1024

F32 = jnp.float32
BF16 = jnp.bfloat16


def dot(left, right, left_dim, right_dim):
    return lax.dot_general(
        left, right, (((left_dim,), (right_dim,)), ((), ())), preferred_element_type=F32
    )


def vmem():
    return pl.BlockSpec(memory_space=pltpu.VMEM)


def smem():
    return pl.BlockSpec(memory_space=pltpu.SMEM)


def call(kernel, out_shape, ins, flops=0, scratch=()):
    size = sum(math.prod(x.shape) * x.dtype.itemsize for x in list(ins) + list(out_shape))
    specs = [smem() if x.dtype == jnp.int32 else vmem() for x in ins]
    return pl.pallas_call(
        kernel,
        out_shape=out_shape,
        in_specs=specs,
        out_specs=[vmem() for _ in out_shape],
        scratch_shapes=list(scratch),
        compiler_params=pltpu.CompilerParams(vmem_limit_bytes=VMEM_LIMIT),
        cost_estimate=pl.CostEstimate(flops=flops, bytes_accessed=size, transcendentals=0),
    )(*ins)


def pack_kernel(q_ref, g_ref, k_ref, v_ref, qg_ref, kv_ref):
    qg_ref[0] = q_ref[...]
    qg_ref[1] = g_ref[...]
    kv_ref[0] = k_ref[...]
    kv_ref[1] = v_ref[...]


def masked_scores(place_ref, ids_ref, mask_ref, q_rows, keys_here, key_group, factor):
    unit = keys_here.shape[0]
    half = unit // 2
    queries = q_rows.shape[0]
    first_query = place_ref[0] * SHARE * 2
    key_unit = key_group * SHARE + place_ref[1]
    scores = dot(keys_here, q_rows, 1, 1) * factor
    lane = lax.broadcasted_iota(jnp.int32, (1, half), 1)
    row = lax.broadcasted_iota(jnp.int32, (half, 1), 0)
    halves = []
    for part in range(2):
        key_block = ids_ref[key_unit * 2 + part]
        limits = []
        for block in range(queries // half):
            query_block = ids_ref[first_query + block]
            linked = mask_ref[query_block, key_block] > 0
            start = jnp.where(linked, (query_block - key_block) * half, -2 * half)
            limits.append(lane + start)
        limit = jnp.concatenate(limits, axis=1)
        halves.append(jnp.where(limit >= row, scores[part * half : (part + 1) * half], MASKED))
    return jnp.concatenate(halves, axis=0)


def stats_kernel(units, factor, place_ref, ids_ref, mask_ref, qg_ref, *refs):
    kv_refs, out_ref = refs[:units], refs[units]
    width = qg_ref.shape[-1]
    q_rows = qg_ref[:, 0].reshape(-1, width)
    g_rows = qg_ref[:, 1].reshape(-1, width)
    scores = [
        masked_scores(place_ref, ids_ref, mask_ref, q_rows, kv_refs[u][0], place_ref[2 + u], factor)
        for u in range(units)
    ]
    top = functools.reduce(jnp.maximum, [jnp.max(s, axis=0, keepdims=True) for s in scores])
    top = jnp.maximum(top, FLOOR)
    total = jnp.zeros_like(top)
    weighted = jnp.zeros_like(top)
    for u in range(units):
        weights = jnp.exp2(scores[u] - top)
        total += jnp.sum(weights, axis=0, keepdims=True)
        grads = dot(kv_refs[u][1], g_rows, 1, 1)
        weighted += jnp.sum(weights * grads, axis=0, keepdims=True)
    out_ref[0:1, :] = top
    out_ref[1:2, :] = total
    out_ref[2:3, :] = weighted


def grads_kernel(units, factor, scale, place_ref, ids_ref, mask_ref, qg_ref, stats_ref, *refs):
    kv_refs = refs[:units]
    kv_out_ref, own_ref = refs[units], refs[units + 1]
    far_refs = refs[units + 2 : units + 1 + SHARE]
    dq_ref = refs[-1]
    width = qg_ref.shape[-1]
    sub = width // GROUP
    unit = qg_ref.shape[2]
    q_rows = qg_ref[:, 0].reshape(-1, width)
    g_rows = qg_ref[:, 1].reshape(-1, width)
    tops = [stats_ref[s, 0:1, :] for s in range(SHARE)]
    top = functools.reduce(jnp.maximum, tops)
    scaled = [jnp.exp2(t - top) for t in tops]
    total = sum(stats_ref[s, 1:2, :] * scaled[s] for s in range(SHARE))
    weighted = sum(stats_ref[s, 2:3, :] * scaled[s] for s in range(SHARE))
    log_total = top + jnp.log2(total)
    delta = weighted / total
    dq = None
    for u in range(units):
        keys_here, values_here = kv_refs[u][0], kv_refs[u][1]
        key_group = place_ref[2 + u]
        scores = masked_scores(place_ref, ids_ref, mask_ref, q_rows, keys_here, key_group, factor)
        probs = jnp.exp2(scores - log_total)
        dprobs = dot(values_here, g_rows, 1, 1)
        dscores = (probs * (dprobs - delta)).astype(BF16)
        dv = dot(probs.astype(BF16), g_rows, 1, 0)
        dk = dot(dscores, q_rows, 1, 0) * scale
        dk = dk.T.astype(BF16)
        dv = dv.T.astype(BF16)
        for part in range(GROUP):
            kv_out_ref[key_group, part, 0] = dk[part * sub : (part + 1) * sub]
            kv_out_ref[key_group, part, 1] = dv[part * sub : (part + 1) * sub]
        term = dot(keys_here, dscores, 0, 0)
        dq = term if dq is None else dq + term
    dq = dq * scale
    for s in range(SHARE):
        dq_ref[s] = dq[:, s * unit : (s + 1) * unit]
    me = place_ref[1]
    own_ref[...] = dq_ref[me]
    for step in range(1, SHARE):
        far_refs[step - 1][...] = dq_ref[me ^ step].astype(BF16)


def final_kernel(own_ref, *refs):
    far_refs = refs[: SHARE - 1]
    kv_ref, dq_ref, dk_ref, dv_ref = refs[SHARE - 1 :]
    dq = own_ref[...]
    for ref in far_refs:
        dq += ref[...].astype(F32)
    dq_ref[...] = dq.T
    for which, out_ref in ((0, dk_ref), (1, dv_ref)):
        total = kv_ref[0, which].astype(F32)
        for source in range(1, kv_ref.shape[0]):
            total += kv_ref[source, which].astype(F32)
        out_ref[...] = total.T


def body(queries, keys, values, out_grad, block_ids, block_mask):
    unit, width = queries.shape
    ctx_size, lanes = lax.axis_size("ctx"), lax.axis_size("fsdp")
    units = ctx_size // SHARE
    scale = width ** (-0.5)
    factor = scale * math.log2(math.e)
    ctx_index = lax.axis_index("ctx")
    key_group = lax.axis_index("fsdp") // GROUP
    sub = width // GROUP
    if keys.shape[1] != width:
        keys = lax.dynamic_slice_in_dim(keys, key_group * width, width, 1)
        values = lax.dynamic_slice_in_dim(values, key_group * width, width, 1)

    pair = jax.ShapeDtypeStruct((2, unit, width), BF16)
    qg, kv = call(pack_kernel, [pair, pair], [queries, out_grad, keys, values])

    def swap(x, step):
        return lax.ppermute(x, "ctx", [(i, i ^ step) for i in range(ctx_size)])

    own_group, own_place = ctx_index // SHARE, ctx_index % SHARE
    key_groups = [own_group ^ u for u in range(units)]
    place = jnp.stack([own_group, own_place] + key_groups).astype(jnp.int32)
    groups = [list(range(g * SHARE, (g + 1) * SHARE)) for g in range(units)]
    kvs = [kv] + [swap(kv, u * SHARE) for u in range(1, units)]
    qgs = lax.all_gather(qg, "ctx", axis_index_groups=groups)

    rows = SHARE * unit
    product = 2 * rows * units * unit * width
    (stats,) = call(
        functools.partial(stats_kernel, units, factor),
        [jax.ShapeDtypeStruct((3, rows), F32)],
        [place, block_ids, block_mask, qgs] + kvs,
        flops=2 * product,
    )
    all_stats = lax.all_gather(stats, "ctx", axis_index_groups=groups)
    tall = (width, unit)
    outs = call(
        functools.partial(grads_kernel, units, factor, scale),
        [
            jax.ShapeDtypeStruct((units, GROUP, 2, sub, unit), BF16),
            jax.ShapeDtypeStruct(tall, F32),
        ]
        + [jax.ShapeDtypeStruct(tall, BF16)] * (SHARE - 1),
        [place, block_ids, block_mask, qgs, all_stats] + kvs,
        flops=5 * product,
        scratch=[pltpu.VMEM((SHARE,) + tall, F32)],
    )
    kv_parts, own, far = outs[0], outs[1], outs[2:]
    far = [swap(x, step + 1) for step, x in enumerate(far)]
    places = [
        [(g * SHARE + s) * lanes + head * GROUP + h for g in range(units) for h in range(GROUP)]
        for s in range(SHARE)
        for head in range(lanes // GROUP)
    ]
    kv_parts = kv_parts.reshape(units * GROUP, 2, sub, unit)
    kv_parts = lax.all_to_all(
        kv_parts, ("ctx", "fsdp"), 0, 0, axis_index_groups=places, tiled=True
    )
    return tuple(
        call(
            final_kernel,
            [
                jax.ShapeDtypeStruct((unit, width), F32),
                jax.ShapeDtypeStruct((unit, sub), F32),
                jax.ShapeDtypeStruct((unit, sub), F32),
            ],
            [own] + far + [kv_parts],
        )
    )


def solution(mesh):
    in_specs = (P("ctx", "fsdp"), P("ctx", None), P("ctx", None), P("ctx", "fsdp"), P(), P())
    out_specs = (P("ctx", "fsdp"), P("ctx", "fsdp"), P("ctx", "fsdp"))
    return jax.shard_map(body, mesh=mesh, in_specs=in_specs, out_specs=out_specs, check_vma=False)
```

```python
import functools
import math

import jax
import jax.numpy as jnp
from jax import lax
from jax.experimental import pallas as pl
from jax.experimental.pallas import tpu as pltpu
from jax.sharding import PartitionSpec as P

GROUP = 4
SHARE = 4
MASKED = -1e30
FLOOR = -1e20
VMEM_LIMIT = 48 * 1024 * 1024
PACK_LIMIT = 65400 * 1024

F32 = jnp.float32
BF16 = jnp.bfloat16


def dot(left, right, left_dim, right_dim):
    return lax.dot_general(
        left, right, (((left_dim,), (right_dim,)), ((), ())), preferred_element_type=F32
    )


def vmem():
    return pl.BlockSpec(memory_space=pltpu.VMEM)


def call(kernel, out_shape, ins, in_specs=None, out_specs=None, flops=0, scratch=(), limit=VMEM_LIMIT):
    size = sum(math.prod(x.shape) * x.dtype.itemsize for x in list(ins) + list(out_shape))
    return pl.pallas_call(
        kernel,
        out_shape=out_shape,
        in_specs=in_specs or [vmem() for _ in ins],
        out_specs=out_specs or [vmem() for _ in out_shape],
        scratch_shapes=list(scratch),
        compiler_params=pltpu.CompilerParams(vmem_limit_bytes=limit),
        cost_estimate=pl.CostEstimate(flops=flops, bytes_accessed=size, transcendentals=0),
    )(*ins)


def pack_kernel(
    units, q_ref, g_ref, k_ref, v_ref, ids_ref, mask_ref, qg_ref, kv_ref, limit_ref, ids, mask, sems
):
    copies = [
        pltpu.make_async_copy(source, target, sems.at[i])
        for i, (source, target) in enumerate(
            [
                (ids_ref, ids),
                (mask_ref, mask),
                (k_ref, kv_ref.at[0]),
                (v_ref, kv_ref.at[1]),
                (q_ref, qg_ref.at[0]),
                (g_ref, qg_ref.at[1]),
            ]
        )
    ]
    for copy in copies:
        copy.start()
    half = k_ref.shape[0] // 2
    ctx_index = lax.axis_index("ctx")
    group, place = ctx_index // SHARE, ctx_index % SHARE
    lane = lax.broadcasted_iota(jnp.int32, (1, half), 1)
    copies[0].wait()
    copies[1].wait()
    query_blocks = [ids[group * SHARE * 2 + i] for i in range(SHARE * 2)]
    for u in range(units):
        for part in range(2):
            key_block = ids[((group ^ u) * SHARE + place) * 2 + part]
            row = u * 2 + part
            for i, query_block in enumerate(query_blocks):
                linked = mask[query_block, key_block] > 0
                start = jnp.where(linked, (query_block - key_block) * half, -2 * half)
                limit_ref[row : row + 1, i * half : (i + 1) * half] = lane + start
    for copy in copies[2:]:
        copy.wait()


def masked_scores(limit_ref, q_rows, keys_here, u, factor):
    half = keys_here.shape[0] // 2
    scores = dot(keys_here, q_rows, 1, 1) * factor
    row = lax.broadcasted_iota(jnp.int32, (half, 1), 0)
    halves = [
        jnp.where(
            limit_ref[u * 2 + part : u * 2 + part + 1, :] >= row,
            scores[part * half : (part + 1) * half],
            MASKED,
        )
        for part in range(2)
    ]
    return jnp.concatenate(halves, axis=0)


def stats_kernel(units, factor, limit_ref, qg_ref, *refs):
    kv_refs, out_ref = refs[:units], refs[units]
    width = qg_ref.shape[-1]
    q_rows = qg_ref[:, 0].reshape(-1, width)
    g_rows = qg_ref[:, 1].reshape(-1, width)
    scores = [masked_scores(limit_ref, q_rows, kv_refs[u][0], u, factor) for u in range(units)]
    top = functools.reduce(jnp.maximum, [jnp.max(s, axis=0, keepdims=True) for s in scores])
    top = jnp.maximum(top, FLOOR)
    total = jnp.zeros_like(top)
    weighted = jnp.zeros_like(top)
    for u in range(units):
        weights = jnp.exp2(scores[u] - top)
        total += jnp.sum(weights, axis=0, keepdims=True)
        grads = dot(kv_refs[u][1], g_rows, 1, 1)
        weighted += jnp.sum(weights * grads, axis=0, keepdims=True)
    out_ref[0:1, :] = top
    out_ref[1:2, :] = total
    out_ref[2:3, :] = weighted


def grads_kernel(units, factor, scale, limit_ref, qg_ref, stats_ref, *refs):
    kv_refs = refs[:units]
    kv_out_ref, ds_ref = refs[units:]
    width = qg_ref.shape[-1]
    sub = width // GROUP
    unit = qg_ref.shape[2]
    q_rows = qg_ref[:, 0].reshape(-1, width)
    g_rows = qg_ref[:, 1].reshape(-1, width)
    tops = [stats_ref[s, 0:1, :] for s in range(SHARE)]
    top = functools.reduce(jnp.maximum, tops)
    scaled = [jnp.exp2(t - top) for t in tops]
    total = sum(stats_ref[s, 1:2, :] * scaled[s] for s in range(SHARE))
    weighted = sum(stats_ref[s, 2:3, :] * scaled[s] for s in range(SHARE))
    log_total = top + jnp.log2(total)
    delta = weighted / total
    group = lax.axis_index("ctx") // SHARE
    for u in range(units):
        keys_here, values_here = kv_refs[u][0], kv_refs[u][1]
        scores = masked_scores(limit_ref, q_rows, keys_here, u, factor)
        probs = jnp.exp2(scores - log_total)
        dprobs = dot(values_here, g_rows, 1, 1)
        dscores = (probs * (dprobs - delta)).astype(BF16)
        ds_ref[u * unit : (u + 1) * unit] = dscores
        dv = dot(probs.astype(BF16), g_rows, 1, 0)
        dk = dot(dscores, q_rows, 1, 0) * scale
        dk = dk.T.astype(BF16)
        dv = dv.T.astype(BF16)
        for part in range(GROUP):
            kv_out_ref[group ^ u, part, 0] = dk[part * sub : (part + 1) * sub]
            kv_out_ref[group ^ u, part, 1] = dv[part * sub : (part + 1) * sub]


def query_kernel(units, scale, ds_ref, *refs):
    kv_refs, own_ref, far_refs = refs[:units], refs[units], refs[units + 1 : units + SHARE]
    dq_ref = refs[-1]
    unit = own_ref.shape[0]
    dq = sum(
        dot(kv_refs[u][0], ds_ref[u * unit : (u + 1) * unit], 0, 0) for u in range(units)
    )
    dq = (dq * scale).T
    for s in range(SHARE):
        dq_ref[s] = dq[s * unit : (s + 1) * unit]
    me = lax.axis_index("ctx") % SHARE
    own_ref[...] = dq_ref[me]
    for step in range(1, SHARE):
        far_refs[step - 1][...] = dq_ref[me ^ step].astype(BF16)


def final_kernel(own_ref, *refs):
    far_refs = refs[: SHARE - 1]
    kv_ref, dq_ref, dk_ref, dv_ref = refs[SHARE - 1 :]
    dq = own_ref[...]
    for ref in far_refs:
        dq += ref[...].astype(F32)
    dq_ref[...] = dq
    for which, out_ref in ((0, dk_ref), (1, dv_ref)):
        total = kv_ref[0, which].astype(F32)
        for source in range(1, kv_ref.shape[0]):
            total += kv_ref[source, which].astype(F32)
        out_ref[...] = total


def body(queries, keys, values, out_grad, block_ids, block_mask):
    unit, width = queries.shape
    ctx_size, lanes = lax.axis_size("ctx"), lax.axis_size("fsdp")
    units = ctx_size // SHARE
    rows = SHARE * unit
    sub = width // GROUP
    scale = width ** (-0.5)
    factor = scale * math.log2(math.e)
    if keys.shape[1] != width:
        key_group = lax.axis_index("fsdp") // GROUP
        keys = lax.dynamic_slice_in_dim(keys, key_group * width, width, 1)
        values = lax.dynamic_slice_in_dim(values, key_group * width, width, 1)

    def swap(x, step):
        return lax.ppermute(x, "ctx", [(i, i ^ step) for i in range(ctx_size)])

    pair = jax.ShapeDtypeStruct((2, unit, width), BF16)
    qg, kv, limits = call(
        functools.partial(pack_kernel, units),
        [pair, pair, jax.ShapeDtypeStruct((2 * units, rows), jnp.int32)],
        [queries, out_grad, keys, values, block_ids, block_mask],
        in_specs=[pl.BlockSpec(memory_space=pl.ANY)] * 6,
        limit=PACK_LIMIT,
        scratch=[
            pltpu.SMEM(block_ids.shape, jnp.int32),
            pltpu.SMEM(block_mask.shape, jnp.int32),
            pltpu.SemaphoreType.DMA((6,)),
        ],
    )
    groups = [list(range(g * SHARE, (g + 1) * SHARE)) for g in range(units)]
    kvs = [kv] + [swap(kv, u * SHARE) for u in range(1, units)]
    qgs = lax.all_gather(qg, "ctx", axis_index_groups=groups)

    product = 2 * rows * units * unit * width
    (stats,) = call(
        functools.partial(stats_kernel, units, factor),
        [jax.ShapeDtypeStruct((3, rows), F32)],
        [limits, qgs] + kvs,
        flops=2 * product,
    )
    all_stats = lax.all_gather(stats, "ctx", axis_index_groups=groups)
    kv_parts, dscores = call(
        functools.partial(grads_kernel, units, factor, scale),
        [
            jax.ShapeDtypeStruct((units, GROUP, 2, sub, unit), BF16),
            jax.ShapeDtypeStruct((units * unit, rows), BF16),
        ],
        [limits, qgs, all_stats] + kvs,
        flops=4 * product,
    )
    places = [
        [(g * SHARE + s) * lanes + head * GROUP + h for g in range(units) for h in range(GROUP)]
        for s in range(SHARE)
        for head in range(lanes // GROUP)
    ]
    kv_parts = kv_parts.reshape(units * GROUP, 2, sub, unit)
    kv_parts = lax.all_to_all(
        kv_parts, ("ctx", "fsdp"), 0, 0, axis_index_groups=places, tiled=True
    )
    own, *far = call(
        functools.partial(query_kernel, units, scale),
        [jax.ShapeDtypeStruct((unit, width), F32)]
        + [jax.ShapeDtypeStruct((unit, width), BF16)] * (SHARE - 1),
        [dscores] + kvs,
        flops=product,
        scratch=[pltpu.VMEM((SHARE, unit, width), F32)],
    )
    far = [swap(x, step + 1) for step, x in enumerate(far)]
    dq, dk, dv = call(
        final_kernel,
        [
            jax.ShapeDtypeStruct((unit, width), F32),
            jax.ShapeDtypeStruct((sub, unit), F32),
            jax.ShapeDtypeStruct((sub, unit), F32),
        ],
        [own] + far + [kv_parts],
    )
    return dq, dk.T, dv.T


def solution(mesh):
    in_specs = (P("ctx", "fsdp"), P("ctx", None), P("ctx", None), P("ctx", "fsdp"), P(), P())
    out_specs = (P("ctx", "fsdp"), P("ctx", "fsdp"), P("ctx", "fsdp"))
    return jax.shard_map(body, mesh=mesh, in_specs=in_specs, out_specs=out_specs, check_vma=False)
```

```python
import functools
import math

import jax
import jax.numpy as jnp
from jax import lax
from jax.experimental import pallas as pl
from jax.experimental.pallas import tpu as pltpu
from jax.sharding import PartitionSpec as P

GROUP = 4
SHARE = 4
MASKED = -1e30
FLOOR = -1e20
VMEM_LIMIT = 48 * 1024 * 1024

F32 = jnp.float32
BF16 = jnp.bfloat16


def dot(left, right, left_dim, right_dim):
    return lax.dot_general(
        left, right, (((left_dim,), (right_dim,)), ((), ())), preferred_element_type=F32
    )


def vmem():
    return pl.BlockSpec(memory_space=pltpu.VMEM)


def call(kernel, out_shape, ins, in_specs=None, flops=0, scratch=()):
    size = sum(math.prod(x.shape) * x.dtype.itemsize for x in list(ins) + list(out_shape))
    return pl.pallas_call(
        kernel,
        out_shape=out_shape,
        in_specs=in_specs or [vmem() for _ in ins],
        out_specs=[vmem() for _ in out_shape],
        scratch_shapes=list(scratch),
        compiler_params=pltpu.CompilerParams(vmem_limit_bytes=VMEM_LIMIT),
        cost_estimate=pl.CostEstimate(flops=flops, bytes_accessed=size, transcendentals=0),
    )(*ins)


def limits_kernel(units, half, ids_ref, mask_ref, limit_ref):
    ctx_index = lax.axis_index("ctx")
    lane = lax.broadcasted_iota(jnp.int32, (1, half), 1)
    query_blocks = [ids_ref[(ctx_index ^ r) * 2 + part] for r in range(SHARE) for part in range(2)]
    for u in range(units):
        for part in range(2):
            key_block = ids_ref[(ctx_index ^ (u * SHARE)) * 2 + part]
            row = u * 2 + part
            for i, query_block in enumerate(query_blocks):
                linked = mask_ref[query_block, key_block] > 0
                start = jnp.where(linked, (query_block - key_block) * half, -2 * half)
                limit_ref[row : row + 1, i * half : (i + 1) * half] = lane + start


def masked_scores(limit_ref, q_rows, keys_here, u, r, factor):
    unit = keys_here.shape[0]
    half = unit // 2
    scores = dot(keys_here, q_rows, 1, 1) * factor
    row = lax.broadcasted_iota(jnp.int32, (half, 1), 0)
    halves = [
        jnp.where(
            limit_ref[u * 2 + part : u * 2 + part + 1, r * unit : (r + 1) * unit] >= row,
            scores[part * half : (part + 1) * half],
            MASKED,
        )
        for part in range(2)
    ]
    return jnp.concatenate(halves, axis=0)


def stats_kernel(units, factor, limit_ref, *refs):
    qg_refs, kv_refs, out_ref = refs[:SHARE], refs[SHARE:-1], refs[-1]
    me = lax.axis_index("ctx") % SHARE
    for r in range(SHARE):
        q_rows, g_rows = qg_refs[r][0], qg_refs[r][1]
        scores = [masked_scores(limit_ref, q_rows, kv_refs[u][0], u, r, factor) for u in range(units)]
        top = functools.reduce(jnp.maximum, [jnp.max(s, axis=0, keepdims=True) for s in scores])
        top = jnp.maximum(top, FLOOR)
        total = jnp.zeros_like(top)
        weighted = jnp.zeros_like(top)
        for u in range(units):
            weights = jnp.exp2(scores[u] - top)
            total += jnp.sum(weights, axis=0, keepdims=True)
            dprobs = dot(kv_refs[u][1], g_rows, 1, 1)
            weighted += jnp.sum(weights * dprobs, axis=0, keepdims=True)
        out_ref[me ^ r, 0:1, :] = top
        out_ref[me ^ r, 1:2, :] = total
        out_ref[me ^ r, 2:3, :] = weighted


def grads_kernel(wanted, factor, scale, limit_ref, stats_ref, *refs):
    qg_refs, refs = refs[:SHARE], refs[SHARE:]
    kv_refs, ds_ref, out_refs = refs[: len(wanted)], refs[len(wanted)], refs[len(wanted) + 1 :]
    _, unit, width = qg_refs[0].shape
    sub = width // GROUP
    me = lax.axis_index("ctx") % SHARE
    dk, dv = [None] * len(wanted), [None] * len(wanted)
    for r in range(SHARE):
        tops = [stats_ref[s, me ^ r, 0:1, :] for s in range(SHARE)]
        top = functools.reduce(jnp.maximum, tops)
        scaled = [jnp.exp2(t - top) for t in tops]
        total = sum(stats_ref[s, me ^ r, 1:2, :] * scaled[s] for s in range(SHARE))
        weighted = sum(stats_ref[s, me ^ r, 2:3, :] * scaled[s] for s in range(SHARE))
        log_total = top + jnp.log2(total)
        delta = weighted / total
        q_rows, g_rows = qg_refs[r][0], qg_refs[r][1]
        for i, u in enumerate(wanted):
            scores = masked_scores(limit_ref, q_rows, kv_refs[i][0], u, r, factor)
            probs = jnp.exp2(scores - log_total)
            dprobs = dot(kv_refs[i][1], g_rows, 1, 1)
            dscores = (probs * (dprobs - delta)).astype(BF16)
            ds_ref[i * unit : (i + 1) * unit, r * unit : (r + 1) * unit] = dscores
            dv_term = dot(probs.astype(BF16), g_rows, 1, 0)
            dk_term = dot(dscores, q_rows, 1, 0)
            dv[i] = dv_term if r == 0 else dv[i] + dv_term
            dk[i] = dk_term if r == 0 else dk[i] + dk_term
    for i, out_ref in enumerate(out_refs):
        dk_tall = (dk[i] * scale).T.astype(out_ref.dtype)
        dv_tall = dv[i].T.astype(out_ref.dtype)
        for part in range(GROUP):
            out_ref[part, 0] = dk_tall[part * sub : (part + 1) * sub]
            out_ref[part, 1] = dv_tall[part * sub : (part + 1) * sub]


def merge_kernel(*refs):
    terms, total_ref, (own_ref, *far_refs) = refs[: -GROUP - 1], refs[-1], refs[-GROUP - 1 : -1]
    total_ref[...] = sum(ref[...].astype(F32) for ref in terms)
    lane = lax.axis_index("fsdp") % GROUP
    own_ref[...] = total_ref[lane]
    for h in range(1, GROUP):
        far_refs[h - 1][...] = total_ref[lane ^ h].astype(BF16)


def query_kernel(units, scale, near_ref, far_ref, *refs):
    kv_refs, own_ref, far_refs = refs[:units], refs[units], refs[units + 1 :]
    unit = own_ref.shape[0]
    dq = dot(kv_refs[0][0], near_ref[...], 0, 0)
    for u in range(1, units):
        dq += dot(kv_refs[u][0], far_ref[(u - 1) * unit : u * unit], 0, 0)
    dq = (dq * scale).T
    own_ref[...] = dq[:unit]
    for r in range(1, SHARE):
        far_refs[r - 1][...] = dq[r * unit : (r + 1) * unit].astype(BF16)


def final_kernel(own_ref, *refs):
    far_refs = refs[: SHARE - 1]
    kv_refs, (dq_ref, dk_ref, dv_ref) = refs[SHARE - 1 : -3], refs[-3:]
    dq = own_ref[...]
    for ref in far_refs:
        dq += ref[...].astype(F32)
    dq_ref[...] = dq
    for which, out_ref in ((0, dk_ref), (1, dv_ref)):
        out_ref[...] = sum(ref[which].astype(F32) for ref in kv_refs)


def body(queries, keys, values, out_grad, block_ids, block_mask):
    unit, width = queries.shape
    ctx_size, lanes = lax.axis_size("ctx"), lax.axis_size("fsdp")
    units = ctx_size // SHARE
    rows = SHARE * unit
    sub = width // GROUP
    scale = width ** (-0.5)
    factor = scale * math.log2(math.e)
    if keys.shape[1] != width:
        key_group = lax.axis_index("fsdp") // GROUP
        keys = lax.dynamic_slice_in_dim(keys, key_group * width, width, 1)
        values = lax.dynamic_slice_in_dim(values, key_group * width, width, 1)

    def swap(x, step):
        return lax.ppermute(x, "ctx", [(i, i ^ step) for i in range(ctx_size)])

    def others(x):
        beyond = swap(x, 2)
        return [x, swap(x, 1), beyond, swap(beyond, 1)]

    qg, kv = jnp.stack([queries, out_grad]), jnp.stack([keys, values])
    qgs = others(qg)
    kvs = [kv] + [swap(kv, u * SHARE) for u in range(1, units)]
    (limits,) = call(
        functools.partial(limits_kernel, units, unit // 2),
        [jax.ShapeDtypeStruct((2 * units, rows), jnp.int32)],
        [block_ids, block_mask],
        in_specs=[pl.BlockSpec(memory_space=pltpu.SMEM)] * 2,
    )
    groups = [list(range(g * SHARE, (g + 1) * SHARE)) for g in range(units)]
    operands = qgs + kvs
    product = 2 * rows * units * unit * width
    (stats,) = call(
        functools.partial(stats_kernel, units, factor),
        [jax.ShapeDtypeStruct((SHARE, 3, unit), F32)],
        [limits] + operands,
        flops=2 * product,
    )
    all_stats = lax.all_gather(stats, "ctx", axis_index_groups=groups)
    spread = (GROUP, 2, sub, unit)
    far_scores, *far_parts = call(
        functools.partial(grads_kernel, list(range(1, units)), factor, scale),
        [jax.ShapeDtypeStruct(((units - 1) * unit, rows), BF16)]
        + [jax.ShapeDtypeStruct(spread, BF16)] * (units - 1),
        [limits, all_stats] + qgs + kvs[1:],
        flops=4 * product,
    )
    far_parts = [swap(x, (u + 1) * SHARE) for u, x in enumerate(far_parts)]
    near_scores, near_part = call(
        functools.partial(grads_kernel, [0], factor, scale),
        [jax.ShapeDtypeStruct((unit, rows), BF16), jax.ShapeDtypeStruct(spread, F32)],
        [limits, all_stats] + qgs + kvs[:1],
        flops=4 * product,
    )
    own, *far = call(
        functools.partial(query_kernel, units, scale),
        [jax.ShapeDtypeStruct((unit, width), F32)]
        + [jax.ShapeDtypeStruct((unit, width), BF16)] * (SHARE - 1),
        [near_scores, far_scores] + kvs,
        flops=product,
    )
    far = [swap(x, step + 1) for step, x in enumerate(far)]
    def cross(x, step):
        return lax.ppermute(x, "fsdp", [(i, i ^ step) for i in range(lanes)])

    own_part, *others_part = call(
        merge_kernel,
        [jax.ShapeDtypeStruct(spread[1:], F32)]
        + [jax.ShapeDtypeStruct(spread[1:], BF16)] * (GROUP - 1),
        [near_part] + far_parts,
        scratch=[pltpu.VMEM(spread, F32)],
    )
    parts = [own_part] + [cross(others_part[h - 1], h) for h in reversed(range(1, GROUP))]
    dq, dk, dv = call(
        final_kernel,
        [
            jax.ShapeDtypeStruct((unit, width), F32),
            jax.ShapeDtypeStruct((sub, unit), F32),
            jax.ShapeDtypeStruct((sub, unit), F32),
        ],
        [own] + far + parts,
    )
    return dq, dk.T, dv.T


def solution(mesh):
    in_specs = (P("ctx", "fsdp"), P("ctx", None), P("ctx", None), P("ctx", "fsdp"), P(), P())
    out_specs = (P("ctx", "fsdp"), P("ctx", "fsdp"), P("ctx", "fsdp"))
    return jax.shard_map(body, mesh=mesh, in_specs=in_specs, out_specs=out_specs, check_vma=False)
```

```python
import functools
import math

import jax
import jax.numpy as jnp
from jax import lax
from jax.experimental import pallas as pl
from jax.experimental.pallas import tpu as pltpu
from jax.sharding import PartitionSpec as P

GROUP = 4
SHARE = 4
MASKED = -1e30
FLOOR = -1e20
VMEM_LIMIT = 48 * 1024 * 1024

F32 = jnp.float32
BF16 = jnp.bfloat16


def dot(left, right, left_dim, right_dim):
    return lax.dot_general(
        left, right, (((left_dim,), (right_dim,)), ((), ())), preferred_element_type=F32
    )


def vmem():
    return pl.BlockSpec(memory_space=pltpu.VMEM)


def call(kernel, out_shape, ins, in_specs=None, flops=0, scratch=()):
    size = sum(math.prod(x.shape) * x.dtype.itemsize for x in list(ins) + list(out_shape))
    return pl.pallas_call(
        kernel,
        out_shape=out_shape,
        in_specs=in_specs or [vmem() for _ in ins],
        out_specs=[vmem() for _ in out_shape],
        scratch_shapes=list(scratch),
        compiler_params=pltpu.CompilerParams(vmem_limit_bytes=VMEM_LIMIT),
        cost_estimate=pl.CostEstimate(flops=flops, bytes_accessed=size, transcendentals=0),
    )(*ins)


def limits_kernel(units, half, ids_ref, mask_ref, *limit_refs):
    ctx_index = lax.axis_index("ctx")
    lane = lax.broadcasted_iota(jnp.int32, (1, half), 1)
    for r, limit_ref in enumerate(limit_refs):
        for side in range(2):
            query_block = ids_ref[(ctx_index ^ r) * 2 + side]
            for row in range(2 * units):
                key_block = ids_ref[(ctx_index ^ (row // 2 * SHARE)) * 2 + row % 2]
                linked = mask_ref[query_block, key_block] > 0
                start = jnp.where(linked, (query_block - key_block) * half, -2 * half)
                limit_ref[row : row + 1, side * half : (side + 1) * half] = lane + start


def after_kernel(in_ref, after_ref, out_ref):
    del after_ref
    out_ref[...] = in_ref[...]


def unit_kernel(units, factor, limit_ref, qg_ref, *refs):
    kv_refs, (exp_ref, dprob_ref, stats_ref) = refs[:units], refs[units:]
    unit = qg_ref.shape[1]
    half = unit // 2
    q_rows, g_rows = qg_ref[0], qg_ref[1]
    row = lax.broadcasted_iota(jnp.int32, (half, 1), 0)
    scores = []
    for u in range(units):
        products = dot(kv_refs[u][0], q_rows, 1, 1) * factor
        for part in range(2):
            allowed = limit_ref[u * 2 + part : u * 2 + part + 1, :] >= row
            scores.append(jnp.where(allowed, products[part * half : (part + 1) * half], MASKED))
    top = functools.reduce(jnp.maximum, [jnp.max(s, axis=0, keepdims=True) for s in scores])
    top = jnp.maximum(top, FLOOR)
    total = jnp.zeros_like(top)
    weighted = jnp.zeros_like(top)
    for u in range(units):
        dprobs = dot(kv_refs[u][1], g_rows, 1, 1)
        for part in range(2):
            start = u * unit + part * half
            weights = jnp.exp2(scores[u * 2 + part] - top)
            here = dprobs[part * half : (part + 1) * half]
            exp_ref[start : start + half] = weights
            dprob_ref[start : start + half] = here
            total += jnp.sum(weights, axis=0, keepdims=True)
            weighted += jnp.sum(weights * here, axis=0, keepdims=True)
    stats_ref[0:1, :] = top
    stats_ref[1:2, :] = total
    stats_ref[2:3, :] = weighted


def collect_kernel(*refs):
    for r in range(SHARE):
        refs[-1][r] = refs[r][...]


def merge_stats(left, right):
    top = jnp.maximum(left[0:1], right[0:1])
    first, second = jnp.exp2(left[0:1] - top), jnp.exp2(right[0:1] - top)
    return (
        top,
        left[1:2] * first + right[1:2] * second,
        left[2:3] * first + right[2:3] * second,
    )


def pair_kernel(own_ref, other_ref, out_ref):
    for r in range(SHARE):
        for row, value in enumerate(merge_stats(own_ref[r], other_ref[r ^ 1])):
            out_ref[r, row : row + 1, :] = value


def grads_kernel(u, scale, *refs):
    (own_ref, near_ref, far_ref), refs = refs[:3], refs[3:]
    qg_refs, refs = refs[:SHARE], refs[SHARE:]
    exp_refs, dprob_refs = refs[:SHARE], refs[SHARE : 2 * SHARE]
    ds_ref, out_ref = refs[2 * SHARE :]
    _, unit, width = qg_refs[0].shape
    sub = width // GROUP
    dk, dv = 0.0, 0.0
    for r in range(SHARE):
        top, total, weighted = merge_stats(near_ref[r], far_ref[r ^ 2])
        share = jnp.exp2(own_ref[r, 0:1] - top) / total
        delta = weighted / total
        probs = exp_refs[r][u * unit : (u + 1) * unit] * share
        dprobs = dprob_refs[r][u * unit : (u + 1) * unit]
        dscores = (probs * (dprobs - delta)).astype(BF16)
        ds_ref[:, r * unit : (r + 1) * unit] = dscores
        dv += dot(probs.astype(BF16), qg_refs[r][1], 1, 0)
        dk += dot(dscores, qg_refs[r][0], 1, 0)
    dk_tall = (dk * scale).T.astype(out_ref.dtype)
    dv_tall = dv.T.astype(out_ref.dtype)
    for part in range(GROUP):
        out_ref[part, 0] = dk_tall[part * sub : (part + 1) * sub]
        out_ref[part, 1] = dv_tall[part * sub : (part + 1) * sub]


def merge_kernel(*refs):
    terms, total_ref, (own_ref, *far_refs) = refs[: -GROUP - 1], refs[-1], refs[-GROUP - 1 : -1]
    total_ref[...] = sum(ref[...].astype(F32) for ref in terms)
    lane = lax.axis_index("fsdp") % GROUP
    own_ref[...] = total_ref[lane]
    for h in range(1, GROUP):
        far_refs[h - 1][...] = total_ref[(lane + h) % GROUP].astype(BF16)


def query_kernel(units, scale, *refs):
    ds_refs, kv_refs = refs[:units], refs[units : 2 * units]
    own_ref, far_refs = refs[2 * units], refs[2 * units + 1 :]
    unit = own_ref.shape[0]
    dq = sum(dot(kv_refs[u][0], ds_refs[u][...], 0, 0) for u in range(units))
    dq = (dq * scale).T
    own_ref[...] = dq[:unit]
    for r in range(1, SHARE):
        far_refs[r - 1][...] = dq[r * unit : (r + 1) * unit].astype(BF16)


def sum_kernel(*refs):
    refs[-1][...] = sum(ref[...].astype(F32) for ref in refs[:-1])


def final_kernel(*refs):
    parts, (dk_ref, dv_ref) = refs[:-2], refs[-2:]
    dk_ref[...] = sum(ref[0].astype(F32) for ref in parts)
    dv_ref[...] = sum(ref[1].astype(F32) for ref in parts)


def body(queries, keys, values, out_grad, block_ids, block_mask):
    unit, width = queries.shape
    ctx_size, lanes = lax.axis_size("ctx"), lax.axis_size("fsdp")
    units = ctx_size // SHARE
    rows = SHARE * unit
    sub = width // GROUP
    scale = width ** (-0.5)
    factor = scale * math.log2(math.e)
    if keys.shape[1] != width:
        key_group = lax.axis_index("fsdp") // GROUP
        keys = lax.dynamic_slice_in_dim(keys, key_group * width, width, 1)
        values = lax.dynamic_slice_in_dim(values, key_group * width, width, 1)

    def swap(x, step):
        return lax.ppermute(x, "ctx", [(i, i ^ step) for i in range(ctx_size)])

    qg, kv = jnp.stack([queries, out_grad]), jnp.stack([keys, values])
    far_qg = swap(qg, 2)
    kvs = [kv] + [swap(kv, u * SHARE) for u in range(1, units)]
    limits = call(
        functools.partial(limits_kernel, units, unit // 2),
        [jax.ShapeDtypeStruct((2 * units, unit), jnp.int32)] * SHARE,
        [block_ids, block_mask],
        in_specs=[pl.BlockSpec(memory_space=pltpu.SMEM)] * 2,
    )
    (sent_qg,) = call(after_kernel, [jax.ShapeDtypeStruct(far_qg.shape, BF16)], [far_qg, limits[0]])
    qgs = [qg, swap(qg, 1), far_qg, swap(sent_qg, 1)]

    product = 2 * unit * unit * width
    grid = jax.ShapeDtypeStruct((units * unit, unit), F32)
    results = [
        call(
            functools.partial(unit_kernel, units, factor),
            [grid, grid, jax.ShapeDtypeStruct((3, unit), F32)],
            [limits[r], qgs[r]] + kvs,
            flops=2 * units * product,
        )
        for r in range(SHARE)
    ]
    exps, dprobs, stats = zip(*results)
    (stats,) = call(
        collect_kernel, [jax.ShapeDtypeStruct((SHARE, 3, unit), F32)], list(stats)
    )
    (chip_stats,) = call(
        pair_kernel, [jax.ShapeDtypeStruct(stats.shape, F32)], [stats, swap(stats, 1)]
    )
    operands = [stats, chip_stats, swap(chip_stats, 2)] + qgs + list(exps) + list(dprobs)

    parts = (GROUP, 2, sub, unit)
    scores, shares = [], []
    for u in reversed(range(units)):
        dscores, share = call(
            functools.partial(grads_kernel, u, scale),
            [
                jax.ShapeDtypeStruct((unit, rows), BF16),
                jax.ShapeDtypeStruct(parts, BF16 if u else F32),
            ],
            operands,
            flops=2 * SHARE * product,
        )
        scores.insert(0, dscores)
        shares.insert(0, swap(share, u * SHARE) if u else share)
    own, *far = call(
        functools.partial(query_kernel, units, scale),
        [jax.ShapeDtypeStruct((unit, width), F32)]
        + [jax.ShapeDtypeStruct((unit, width), BF16)] * (SHARE - 1),
        scores + kvs,
        flops=SHARE * units * product,
    )
    far = [swap(x, step + 1) for step, x in enumerate(far)]

    def cross(x, step):
        pairs = [(i, i // GROUP * GROUP + (i + step) % GROUP) for i in range(lanes)]
        return lax.ppermute(x, "fsdp", pairs)

    own_part, *others_part = call(
        merge_kernel,
        [jax.ShapeDtypeStruct(parts[1:], F32)]
        + [jax.ShapeDtypeStruct(parts[1:], BF16)] * (GROUP - 1),
        shares,
        scratch=[pltpu.VMEM(parts, F32)],
    )
    columns = [own_part] + [cross(others_part[h - 1], h) for h in range(1, GROUP)]
    (dq,) = call(sum_kernel, [jax.ShapeDtypeStruct((unit, width), F32)], [own] + far)
    dk, dv = call(final_kernel, [jax.ShapeDtypeStruct((sub, unit), F32)] * 2, columns)
    return dq, dk.T, dv.T


def solution(mesh):
    in_specs = (P("ctx", "fsdp"), P("ctx", None), P("ctx", None), P("ctx", "fsdp"), P(), P())
    out_specs = (P("ctx", "fsdp"), P("ctx", "fsdp"), P("ctx", "fsdp"))
    return jax.shard_map(body, mesh=mesh, in_specs=in_specs, out_specs=out_specs, check_vma=False)
```

```python
import functools
import math

import jax
import jax.numpy as jnp
from jax import lax
from jax.experimental import pallas as pl
from jax.experimental.pallas import tpu as pltpu
from jax.sharding import PartitionSpec as P

GROUP = 4
SHARE = 4
MASKED = -1e30
FLOOR = -1e20
VMEM_LIMIT = 48 * 1024 * 1024

F32 = jnp.float32
BF16 = jnp.bfloat16


def dot(left, right, left_dim, right_dim):
    return lax.dot_general(
        left, right, (((left_dim,), (right_dim,)), ((), ())), preferred_element_type=F32
    )


def vmem():
    return pl.BlockSpec(memory_space=pltpu.VMEM)


def call(kernel, out_shape, ins, in_specs=None, flops=0, scratch=()):
    size = sum(math.prod(x.shape) * x.dtype.itemsize for x in list(ins) + list(out_shape))
    return pl.pallas_call(
        kernel,
        out_shape=out_shape,
        in_specs=in_specs or [vmem() for _ in ins],
        out_specs=[vmem() for _ in out_shape],
        scratch_shapes=list(scratch),
        compiler_params=pltpu.CompilerParams(vmem_limit_bytes=VMEM_LIMIT),
        cost_estimate=pl.CostEstimate(flops=flops, bytes_accessed=size, transcendentals=0),
    )(*ins)


def limits_kernel(units, half, ids_ref, mask_ref, *limit_refs):
    ctx_index = lax.axis_index("ctx")
    lane = lax.broadcasted_iota(jnp.int32, (1, half), 1)
    for r, limit_ref in enumerate(limit_refs):
        for side in range(2):
            query_block = ids_ref[(ctx_index ^ r) * 2 + side]
            for row in range(2 * units):
                key_block = ids_ref[(ctx_index ^ (row // 2 * SHARE)) * 2 + row % 2]
                linked = mask_ref[query_block, key_block] > 0
                start = jnp.where(linked, (query_block - key_block) * half, -2 * half)
                limit_ref[row : row + 1, side * half : (side + 1) * half] = lane + start


def after_kernel(in_ref, after_ref, out_ref):
    del after_ref
    out_ref[...] = in_ref[...]


def tile_kernel(tiles, factor, *refs):
    count = len(tiles)
    limit_refs, qg_refs, kv_refs = (refs[i * count : (i + 1) * count] for i in range(3))
    exp_refs, dprob_refs, stats_refs = (refs[i * count : (i + 1) * count] for i in range(3, 6))
    unit = qg_refs[0].shape[1]
    half = unit // 2
    row = lax.broadcasted_iota(jnp.int32, (half, 1), 0)
    for i, (_, u) in enumerate(tiles):
        products = dot(kv_refs[i][0], qg_refs[i][0], 1, 1) * factor
        scores = jnp.concatenate(
            [
                jnp.where(
                    limit_refs[i][u * 2 + part : u * 2 + part + 1, :] >= row,
                    products[part * half : (part + 1) * half],
                    MASKED,
                )
                for part in range(2)
            ],
            axis=0,
        )
        top = jnp.maximum(jnp.max(scores, axis=0, keepdims=True), FLOOR)
        weights = jnp.exp2(scores - top)
        dprobs = dot(kv_refs[i][1], qg_refs[i][1], 1, 1)
        exp_refs[i][...] = weights
        dprob_refs[i][...] = dprobs
        stats_refs[i][0:1, :] = top
        stats_refs[i][1:2, :] = jnp.sum(weights, axis=0, keepdims=True)
        stats_refs[i][2:3, :] = jnp.sum(weights * dprobs, axis=0, keepdims=True)


def merge_stats(left, right):
    top = jnp.maximum(left[0:1], right[0:1])
    first, second = jnp.exp2(left[0:1] - top), jnp.exp2(right[0:1] - top)
    return jnp.concatenate(
        [top, left[1:2] * first + right[1:2] * second, left[2:3] * first + right[2:3] * second],
        axis=0,
    )


def collect_kernel(units, *refs):
    for r in range(SHARE):
        stats = functools.reduce(merge_stats, [refs[r * units + u][...] for u in range(units)])
        refs[-1][r] = stats


def grads_kernel(scale, *refs):
    all_refs, refs = refs[:SHARE], refs[SHARE:]
    qg_refs, refs = refs[:SHARE], refs[SHARE:]
    exp_refs, dprob_refs, stats_refs = (refs[i * SHARE : (i + 1) * SHARE] for i in range(3))
    ds_ref, out_ref = refs[3 * SHARE :]
    _, unit, width = qg_refs[0].shape
    sub = width // GROUP
    dk, dv = 0.0, 0.0
    for r in range(SHARE):
        whole = functools.reduce(merge_stats, [all_refs[s][r ^ s] for s in range(SHARE)])
        share = jnp.exp2(stats_refs[r][0:1] - whole[0:1]) / whole[1:2]
        delta = whole[2:3] / whole[1:2]
        probs = exp_refs[r][...] * share
        dprobs = dprob_refs[r][...]
        dscores = (probs * (dprobs - delta)).astype(BF16)
        ds_ref[:, r * unit : (r + 1) * unit] = dscores
        dv += dot(probs.astype(BF16), qg_refs[r][1], 1, 0)
        dk += dot(dscores, qg_refs[r][0], 1, 0)
    dk_tall = (dk * scale).T.astype(out_ref.dtype)
    dv_tall = dv.T.astype(out_ref.dtype)
    for part in range(GROUP):
        out_ref[part, 0] = dk_tall[part * sub : (part + 1) * sub]
        out_ref[part, 1] = dv_tall[part * sub : (part + 1) * sub]


def merge_kernel(*refs):
    terms, total_ref, (own_ref, *far_refs) = refs[: -GROUP - 1], refs[-1], refs[-GROUP - 1 : -1]
    total_ref[...] = sum(ref[...].astype(F32) for ref in terms)
    lane = lax.axis_index("fsdp") % GROUP
    own_ref[...] = total_ref[lane]
    for h in range(1, GROUP):
        far_refs[h - 1][...] = total_ref[(lane + h) % GROUP].astype(BF16)


def query_kernel(units, scale, *refs):
    ds_refs, kv_refs = refs[:units], refs[units : 2 * units]
    own_ref, far_refs = refs[2 * units], refs[2 * units + 1 :]
    unit = own_ref.shape[0]
    dq = sum(dot(kv_refs[u][0], ds_refs[u][...], 0, 0) for u in range(units))
    dq = (dq * scale).T
    own_ref[...] = dq[:unit]
    for r in range(1, SHARE):
        far_refs[r - 1][...] = dq[r * unit : (r + 1) * unit].astype(BF16)


def sum_kernel(*refs):
    refs[-1][...] = sum(ref[...].astype(F32) for ref in refs[:-1])


def final_kernel(*refs):
    parts, (dk_ref, dv_ref) = refs[:-2], refs[-2:]
    dk_ref[...] = sum(ref[0].astype(F32) for ref in parts)
    dv_ref[...] = sum(ref[1].astype(F32) for ref in parts)


def body(queries, keys, values, out_grad, block_ids, block_mask):
    unit, width = queries.shape
    ctx_size, lanes = lax.axis_size("ctx"), lax.axis_size("fsdp")
    units = ctx_size // SHARE
    rows = SHARE * unit
    sub = width // GROUP
    scale = width ** (-0.5)
    factor = scale * math.log2(math.e)
    if keys.shape[1] != width:
        key_group = lax.axis_index("fsdp") // GROUP
        keys = lax.dynamic_slice_in_dim(keys, key_group * width, width, 1)
        values = lax.dynamic_slice_in_dim(values, key_group * width, width, 1)

    def swap(x, step):
        return lax.ppermute(x, "ctx", [(i, i ^ step) for i in range(ctx_size)])

    qg, kv = jnp.stack([queries, out_grad]), jnp.stack([keys, values])
    far_qg = swap(qg, 2)
    kvs = [kv] + [swap(kv, u * SHARE) for u in range(1, units)]
    limits = call(
        functools.partial(limits_kernel, units, unit // 2),
        [jax.ShapeDtypeStruct((2 * units, unit), jnp.int32)] * SHARE,
        [block_ids, block_mask],
        in_specs=[pl.BlockSpec(memory_space=pltpu.SMEM)] * 2,
    )
    (sent_qg,) = call(after_kernel, [jax.ShapeDtypeStruct(far_qg.shape, BF16)], [far_qg, limits[0]])
    qgs = [qg, swap(qg, 1), far_qg, swap(sent_qg, 1)]

    product = 2 * unit * unit * width
    grid = jax.ShapeDtypeStruct((unit, unit), F32)
    rows_out = jax.ShapeDtypeStruct((3, unit), F32)
    results = {}

    def run_tiles(tiles):
        outs = call(
            functools.partial(tile_kernel, tiles, factor),
            [grid] * (2 * len(tiles)) + [rows_out] * len(tiles),
            [limits[r] for r, _ in tiles] + [qgs[r] for r, _ in tiles] + [kvs[u] for _, u in tiles],
            flops=2 * product * len(tiles),
        )
        for i, tile in enumerate(tiles):
            results[tile] = outs[i :: len(tiles)]

    run_tiles([(0, 0), (2, 0)])
    run_tiles([(r, u) for u in range(1, units) for r in (0, 2)])
    run_tiles([(r, u) for u in range(units) for r in (1, 3)])
    (stats,) = call(
        functools.partial(collect_kernel, units),
        [jax.ShapeDtypeStruct((SHARE, 3, unit), F32)],
        [results[r, u][2] for r in range(SHARE) for u in range(units)],
    )
    came = {step: swap(stats, step) for step in (3, 2, 1)}
    both_stats = [stats] + [came[step] for step in range(1, SHARE)]

    parts = (GROUP, 2, sub, unit)
    scores, shares = [], []
    for u in reversed(range(units)):
        dscores, share = call(
            functools.partial(grads_kernel, scale),
            [
                jax.ShapeDtypeStruct((unit, rows), BF16),
                jax.ShapeDtypeStruct(parts, BF16 if u else F32),
            ],
            both_stats + qgs + [results[r, u][i] for i in range(3) for r in range(SHARE)],
            flops=2 * SHARE * product,
        )
        scores.insert(0, dscores)
        shares.insert(0, swap(share, u * SHARE) if u else share)
    own, *far = call(
        functools.partial(query_kernel, units, scale),
        [jax.ShapeDtypeStruct((unit, width), F32)]
        + [jax.ShapeDtypeStruct((unit, width), BF16)] * (SHARE - 1),
        scores + kvs,
        flops=SHARE * units * product,
    )
    far = [swap(x, step + 1) for step, x in enumerate(far)]

    def cross(x, step):
        pairs = [(i, i // GROUP * GROUP + (i + step) % GROUP) for i in range(lanes)]
        return lax.ppermute(x, "fsdp", pairs)

    own_part, *others_part = call(
        merge_kernel,
        [jax.ShapeDtypeStruct(parts[1:], F32)]
        + [jax.ShapeDtypeStruct(parts[1:], BF16)] * (GROUP - 1),
        shares,
        scratch=[pltpu.VMEM(parts, F32)],
    )
    columns = [own_part] + [cross(others_part[h - 1], h) for h in range(1, GROUP)]
    (dq,) = call(sum_kernel, [jax.ShapeDtypeStruct((unit, width), F32)], [own] + far)
    dk, dv = call(final_kernel, [jax.ShapeDtypeStruct((sub, unit), F32)] * 2, columns)
    return dq, dk.T, dv.T


def solution(mesh):
    in_specs = (P("ctx", "fsdp"), P("ctx", None), P("ctx", None), P("ctx", "fsdp"), P(), P())
    out_specs = (P("ctx", "fsdp"), P("ctx", "fsdp"), P("ctx", "fsdp"))
    return jax.shard_map(body, mesh=mesh, in_specs=in_specs, out_specs=out_specs, check_vma=False)
```

```python
import functools
import math

import jax
import jax.numpy as jnp
from jax import lax
from jax.experimental import pallas as pl
from jax.experimental.pallas import tpu as pltpu
from jax.sharding import PartitionSpec as P

GROUP = 4
SHARE = 4
MASKED = -1e30
FLOOR = -1e20
VMEM_LIMIT = 48 * 1024 * 1024

F32 = jnp.float32
BF16 = jnp.bfloat16


def dot(left, right, left_dim, right_dim):
    return lax.dot_general(
        left, right, (((left_dim,), (right_dim,)), ((), ())), preferred_element_type=F32
    )


def vmem():
    return pl.BlockSpec(memory_space=pltpu.VMEM)


def call(kernel, out_shape, ins, in_specs=None, flops=0, scratch=()):
    size = sum(math.prod(x.shape) * x.dtype.itemsize for x in list(ins) + list(out_shape))
    return pl.pallas_call(
        kernel,
        out_shape=out_shape,
        in_specs=in_specs or [vmem() for _ in ins],
        out_specs=[vmem() for _ in out_shape],
        scratch_shapes=list(scratch),
        compiler_params=pltpu.CompilerParams(vmem_limit_bytes=VMEM_LIMIT),
        cost_estimate=pl.CostEstimate(flops=flops, bytes_accessed=size, transcendentals=0),
    )(*ins)


def limits_kernel(units, half, ids_ref, mask_ref, *limit_refs):
    ctx_index = lax.axis_index("ctx")
    lane = lax.broadcasted_iota(jnp.int32, (1, half), 1)
    for r, limit_ref in enumerate(limit_refs):
        for side in range(2):
            query_block = ids_ref[(ctx_index ^ r) * 2 + side]
            for row in range(2 * units):
                key_block = ids_ref[(ctx_index ^ (row // 2 * SHARE)) * 2 + row % 2]
                linked = mask_ref[query_block, key_block] > 0
                start = jnp.where(linked, (query_block - key_block) * half, -2 * half)
                limit_ref[row : row + 1, side * half : (side + 1) * half] = lane + start


def after_kernel(in_ref, after_ref, out_ref):
    del after_ref
    out_ref[...] = in_ref[...]


def tile_kernel(tiles, factor, *refs):
    count = len(tiles)
    limit_refs, qg_refs, kv_refs = (refs[i * count : (i + 1) * count] for i in range(3))
    exp_refs, dprob_refs, stats_refs = (refs[i * count : (i + 1) * count] for i in range(3, 6))
    unit = qg_refs[0].shape[1]
    half = unit // 2
    row = lax.broadcasted_iota(jnp.int32, (half, 1), 0)
    for i, (_, u) in enumerate(tiles):
        products = dot(kv_refs[i][0], qg_refs[i][0], 1, 1) * factor
        scores = jnp.concatenate(
            [
                jnp.where(
                    limit_refs[i][u * 2 + part : u * 2 + part + 1, :] >= row,
                    products[part * half : (part + 1) * half],
                    MASKED,
                )
                for part in range(2)
            ],
            axis=0,
        )
        top = jnp.maximum(jnp.max(scores, axis=0, keepdims=True), FLOOR)
        weights = jnp.exp2(scores - top)
        dprobs = dot(kv_refs[i][1], qg_refs[i][1], 1, 1)
        exp_refs[i][...] = weights
        dprob_refs[i][...] = dprobs
        stats_refs[i][0:1, :] = top
        stats_refs[i][1:2, :] = jnp.sum(weights, axis=0, keepdims=True)
        stats_refs[i][2:3, :] = jnp.sum(weights * dprobs, axis=0, keepdims=True)


def merge_stats(left, right):
    top = jnp.maximum(left[0:1], right[0:1])
    first, second = jnp.exp2(left[0:1] - top), jnp.exp2(right[0:1] - top)
    return jnp.concatenate(
        [top, left[1:2] * first + right[1:2] * second, left[2:3] * first + right[2:3] * second],
        axis=0,
    )


def collect_kernel(units, *refs):
    for r in range(SHARE):
        stats = functools.reduce(merge_stats, [refs[r * units + u][...] for u in range(units)])
        refs[-1][r] = stats


def grads_kernel(scale, *refs):
    all_refs, refs = refs[:SHARE], refs[SHARE:]
    qg_refs, refs = refs[:SHARE], refs[SHARE:]
    exp_refs, dprob_refs, stats_refs = (refs[i * SHARE : (i + 1) * SHARE] for i in range(3))
    ds_ref, out_ref = refs[3 * SHARE :]
    _, unit, width = qg_refs[0].shape
    sub = width // GROUP
    dk, dv = 0.0, 0.0
    for r in range(SHARE):
        whole = functools.reduce(merge_stats, [all_refs[s][r ^ s] for s in range(SHARE)])
        share = jnp.exp2(stats_refs[r][0:1] - whole[0:1]) / whole[1:2]
        delta = whole[2:3] / whole[1:2]
        probs = exp_refs[r][...] * share
        dprobs = dprob_refs[r][...]
        dscores = (probs * (dprobs - delta)).astype(BF16)
        ds_ref[:, r * unit : (r + 1) * unit] = dscores
        dv += dot(probs.astype(BF16), qg_refs[r][1], 1, 0)
        dk += dot(dscores, qg_refs[r][0], 1, 0)
    dk_tall = (dk * scale).T.astype(out_ref.dtype)
    dv_tall = dv.T.astype(out_ref.dtype)
    for part in range(GROUP):
        out_ref[part, 0] = dk_tall[part * sub : (part + 1) * sub]
        out_ref[part, 1] = dv_tall[part * sub : (part + 1) * sub]


TARGETS = ((2, 3, 1, 0), (3, 2, 0, 1), (1, 0, 3, 2))


def target(lane, h):
    place = TARGETS[h - 1][0]
    for i in range(1, GROUP):
        place = jnp.where(lane == i, TARGETS[h - 1][i], place)
    return place


def merge_kernel(*refs):
    terms, total_ref, (own_ref, *far_refs) = refs[: -GROUP - 1], refs[-1], refs[-GROUP - 1 : -1]
    total_ref[...] = sum(ref[...].astype(F32) for ref in terms)
    lane = lax.axis_index("fsdp") % GROUP
    own_ref[...] = total_ref[lane]
    for h in range(1, GROUP):
        far_refs[h - 1][...] = total_ref[target(lane, h)].astype(BF16)


def query_kernel(units, scale, *refs):
    ds_refs, kv_refs = refs[:units], refs[units : 2 * units]
    own_ref, far_refs = refs[2 * units], refs[2 * units + 1 :]
    unit = own_ref.shape[0]
    dq = sum(dot(kv_refs[u][0], ds_refs[u][...], 0, 0) for u in range(units))
    dq = (dq * scale).T
    own_ref[...] = dq[:unit]
    for r in range(1, SHARE):
        far_refs[r - 1][...] = dq[r * unit : (r + 1) * unit].astype(BF16)


def sum_kernel(*refs):
    refs[-1][...] = sum(ref[...].astype(F32) for ref in refs[:-1])


def final_kernel(*refs):
    parts, (dk_ref, dv_ref) = refs[:-2], refs[-2:]
    dk_ref[...] = sum(ref[0].astype(F32) for ref in parts)
    dv_ref[...] = sum(ref[1].astype(F32) for ref in parts)


def body(queries, keys, values, out_grad, block_ids, block_mask):
    unit, width = queries.shape
    ctx_size, lanes = lax.axis_size("ctx"), lax.axis_size("fsdp")
    units = ctx_size // SHARE
    rows = SHARE * unit
    sub = width // GROUP
    scale = width ** (-0.5)
    factor = scale * math.log2(math.e)
    if keys.shape[1] != width:
        key_group = lax.axis_index("fsdp") // GROUP
        keys = lax.dynamic_slice_in_dim(keys, key_group * width, width, 1)
        values = lax.dynamic_slice_in_dim(values, key_group * width, width, 1)

    def swap(x, step):
        return lax.ppermute(x, "ctx", [(i, i ^ step) for i in range(ctx_size)])

    qg, kv = jnp.stack([queries, out_grad]), jnp.stack([keys, values])
    far_qg = swap(qg, 2)
    kvs = [kv] + [swap(kv, u * SHARE) for u in range(1, units)]
    limits = call(
        functools.partial(limits_kernel, units, unit // 2),
        [jax.ShapeDtypeStruct((2 * units, unit), jnp.int32)] * SHARE,
        [block_ids, block_mask],
        in_specs=[pl.BlockSpec(memory_space=pltpu.SMEM)] * 2,
    )
    (sent_qg,) = call(after_kernel, [jax.ShapeDtypeStruct(far_qg.shape, BF16)], [far_qg, limits[0]])
    qgs = [qg, swap(qg, 1), far_qg, swap(sent_qg, 1)]

    product = 2 * unit * unit * width
    grid = jax.ShapeDtypeStruct((unit, unit), F32)
    rows_out = jax.ShapeDtypeStruct((3, unit), F32)
    results = {}

    def run_tiles(tiles):
        outs = call(
            functools.partial(tile_kernel, tiles, factor),
            [grid] * (2 * len(tiles)) + [rows_out] * len(tiles),
            [limits[r] for r, _ in tiles] + [qgs[r] for r, _ in tiles] + [kvs[u] for _, u in tiles],
            flops=2 * product * len(tiles),
        )
        for i, tile in enumerate(tiles):
            results[tile] = outs[i :: len(tiles)]

    run_tiles([(0, 0), (2, 0)])
    run_tiles([(r, u) for u in range(1, units) for r in (0, 2)])
    run_tiles([(r, u) for u in range(units) for r in (1, 3)])
    (stats,) = call(
        functools.partial(collect_kernel, units),
        [jax.ShapeDtypeStruct((SHARE, 3, unit), F32)],
        [results[r, u][2] for r in range(SHARE) for u in range(units)],
    )
    came = {step: swap(stats, step) for step in (3, 2, 1)}
    both_stats = [stats] + [came[step] for step in range(1, SHARE)]

    parts = (GROUP, 2, sub, unit)
    scores, shares = [], []
    for u in reversed(range(units)):
        dscores, share = call(
            functools.partial(grads_kernel, scale),
            [
                jax.ShapeDtypeStruct((unit, rows), BF16),
                jax.ShapeDtypeStruct(parts, BF16 if u else F32),
            ],
            both_stats + qgs + [results[r, u][i] for i in range(3) for r in range(SHARE)],
            flops=2 * SHARE * product,
        )
        scores.insert(0, dscores)
        shares.insert(0, swap(share, u * SHARE) if u else share)
    own, *far = call(
        functools.partial(query_kernel, units, scale),
        [jax.ShapeDtypeStruct((unit, width), F32)]
        + [jax.ShapeDtypeStruct((unit, width), BF16)] * (SHARE - 1),
        scores + kvs,
        flops=SHARE * units * product,
    )
    far = [swap(x, step + 1) for step, x in enumerate(far)]

    def cross(x, step):
        pairs = [(i, i // GROUP * GROUP + TARGETS[step - 1][i % GROUP]) for i in range(lanes)]
        return lax.ppermute(x, "fsdp", pairs)

    own_part, *others_part = call(
        merge_kernel,
        [jax.ShapeDtypeStruct(parts[1:], F32)]
        + [jax.ShapeDtypeStruct(parts[1:], BF16)] * (GROUP - 1),
        shares,
        scratch=[pltpu.VMEM(parts, F32)],
    )
    columns = [own_part] + [cross(others_part[h - 1], h) for h in range(1, GROUP)]
    (dq,) = call(sum_kernel, [jax.ShapeDtypeStruct((unit, width), F32)], [own] + far)
    dk, dv = call(final_kernel, [jax.ShapeDtypeStruct((sub, unit), F32)] * 2, columns)
    return dq, dk.T, dv.T


def solution(mesh):
    in_specs = (P("ctx", "fsdp"), P("ctx", None), P("ctx", None), P("ctx", "fsdp"), P(), P())
    out_specs = (P("ctx", "fsdp"), P("ctx", "fsdp"), P("ctx", "fsdp"))
    return jax.shard_map(body, mesh=mesh, in_specs=in_specs, out_specs=out_specs, check_vma=False)
```

```python
import functools
import math

import jax
import jax.numpy as jnp
from jax import lax
from jax.experimental import pallas as pl
from jax.experimental.pallas import tpu as pltpu
from jax.sharding import PartitionSpec as P

GROUP = 4
SHARE = 4
MASKED = -1e30
FLOOR = -1e20
VMEM_LIMIT = 48 * 1024 * 1024

F32 = jnp.float32
BF16 = jnp.bfloat16


def dot(left, right, left_dim, right_dim):
    return lax.dot_general(
        left, right, (((left_dim,), (right_dim,)), ((), ())), preferred_element_type=F32
    )


def vmem():
    return pl.BlockSpec(memory_space=pltpu.VMEM)


def call(kernel, out_shape, ins, in_specs=None, flops=0, scratch=()):
    size = sum(math.prod(x.shape) * x.dtype.itemsize for x in list(ins) + list(out_shape))
    return pl.pallas_call(
        kernel,
        out_shape=out_shape,
        in_specs=in_specs or [vmem() for _ in ins],
        out_specs=[vmem() for _ in out_shape],
        scratch_shapes=list(scratch),
        compiler_params=pltpu.CompilerParams(vmem_limit_bytes=VMEM_LIMIT),
        cost_estimate=pl.CostEstimate(flops=flops, bytes_accessed=size, transcendentals=0),
    )(*ins)


def limits_kernel(units, half, ids_ref, mask_ref, *limit_refs):
    ctx_index = lax.axis_index("ctx")
    lane = lax.broadcasted_iota(jnp.int32, (1, half), 1)
    for r, limit_ref in enumerate(limit_refs):
        for side in range(2):
            query_block = ids_ref[(ctx_index ^ r) * 2 + side]
            for row in range(2 * units):
                key_block = ids_ref[(ctx_index ^ (row // 2 * SHARE)) * 2 + row % 2]
                linked = mask_ref[query_block, key_block] > 0
                start = jnp.where(linked, (query_block - key_block) * half, -2 * half)
                limit_ref[row : row + 1, side * half : (side + 1) * half] = lane + start


def after_kernel(in_ref, after_ref, out_ref):
    del after_ref
    out_ref[...] = in_ref[...]


def tile_kernel(tiles, factor, *refs):
    count = len(tiles)
    limit_refs, qg_refs, kv_refs = (refs[i * count : (i + 1) * count] for i in range(3))
    exp_refs, dprob_refs, stats_refs = (refs[i * count : (i + 1) * count] for i in range(3, 6))
    unit = qg_refs[0].shape[1]
    half = unit // 2
    row = lax.broadcasted_iota(jnp.int32, (half, 1), 0)
    for i, (_, u) in enumerate(tiles):
        products = dot(kv_refs[i][0], qg_refs[i][0], 1, 1) * factor
        scores = jnp.concatenate(
            [
                jnp.where(
                    limit_refs[i][u * 2 + part : u * 2 + part + 1, :] >= row,
                    products[part * half : (part + 1) * half],
                    MASKED,
                )
                for part in range(2)
            ],
            axis=0,
        )
        top = jnp.maximum(jnp.max(scores, axis=0, keepdims=True), FLOOR)
        weights = jnp.exp2(scores - top)
        dprobs = dot(kv_refs[i][1], qg_refs[i][1], 1, 1)
        exp_refs[i][...] = weights
        dprob_refs[i][...] = dprobs
        stats_refs[i][0:1, :] = top
        stats_refs[i][1:2, :] = jnp.sum(weights, axis=0, keepdims=True)
        stats_refs[i][2:3, :] = jnp.sum(weights * dprobs, axis=0, keepdims=True)


def merge_stats(left, right):
    top = jnp.maximum(left[0:1], right[0:1])
    first, second = jnp.exp2(left[0:1] - top), jnp.exp2(right[0:1] - top)
    return jnp.concatenate(
        [top, left[1:2] * first + right[1:2] * second, left[2:3] * first + right[2:3] * second],
        axis=0,
    )


def collect_kernel(units, *refs):
    for r in range(SHARE):
        stats = functools.reduce(merge_stats, [refs[r * units + u][...] for u in range(units)])
        refs[-1][r] = stats


def grads_kernel(scale, *refs):
    all_refs, refs = refs[:SHARE], refs[SHARE:]
    qg_refs, refs = refs[:SHARE], refs[SHARE:]
    exp_refs, dprob_refs, stats_refs = (refs[i * SHARE : (i + 1) * SHARE] for i in range(3))
    ds_ref, out_ref = refs[3 * SHARE :]
    _, unit, width = qg_refs[0].shape
    sub = width // GROUP
    dk, dv = 0.0, 0.0
    for r in range(SHARE):
        whole = functools.reduce(merge_stats, [all_refs[s][r ^ s] for s in range(SHARE)])
        share = jnp.exp2(stats_refs[r][0:1] - whole[0:1]) / whole[1:2]
        delta = whole[2:3] / whole[1:2]
        probs = exp_refs[r][...] * share
        dprobs = dprob_refs[r][...]
        dscores = (probs * (dprobs - delta)).astype(BF16)
        ds_ref[:, r * unit : (r + 1) * unit] = dscores
        dv += dot(probs.astype(BF16), qg_refs[r][1], 1, 0)
        dk += dot(dscores, qg_refs[r][0], 1, 0)
    dk_tall = (dk * scale).T.astype(out_ref.dtype)
    dv_tall = dv.T.astype(out_ref.dtype)
    for part in range(GROUP):
        out_ref[part, 0] = dk_tall[part * sub : (part + 1) * sub]
        out_ref[part, 1] = dv_tall[part * sub : (part + 1) * sub]


TARGETS = (
    ((2, 3, 1, 0), (3, 2, 0, 1), (1, 0, 3, 2)),
    ((1, 3, 0, 2), (3, 2, 1, 0), (2, 0, 3, 1)),
)


def target(core, lane, h):
    place = 0
    for side in range(2):
        for i in range(GROUP):
            here = (lane == i) & (core == side)
            place = jnp.where(here, TARGETS[side][h - 1][i], place)
    return place


def merge_kernel(*refs):
    terms, total_ref, (own_ref, *far_refs) = refs[: -GROUP - 1], refs[-1], refs[-GROUP - 1 : -1]
    total_ref[...] = sum(ref[...].astype(F32) for ref in terms)
    lane, core = lax.axis_index("fsdp") % GROUP, lax.axis_index("ctx") % 2
    own_ref[...] = total_ref[lane]
    for h in range(1, GROUP):
        far_refs[h - 1][...] = total_ref[target(core, lane, h)].astype(BF16)


def query_kernel(units, scale, *refs):
    ds_refs, kv_refs = refs[:units], refs[units : 2 * units]
    own_ref, far_refs = refs[2 * units], refs[2 * units + 1 :]
    unit = own_ref.shape[0]
    dq = sum(dot(kv_refs[u][0], ds_refs[u][...], 0, 0) for u in range(units))
    dq = (dq * scale).T
    own_ref[...] = dq[:unit]
    for r in range(1, SHARE):
        far_refs[r - 1][...] = dq[r * unit : (r + 1) * unit].astype(BF16)


def sum_kernel(*refs):
    refs[-1][...] = sum(ref[...].astype(F32) for ref in refs[:-1])


def final_kernel(*refs):
    parts, (dk_ref, dv_ref) = refs[:-2], refs[-2:]
    dk_ref[...] = sum(ref[0].astype(F32) for ref in parts)
    dv_ref[...] = sum(ref[1].astype(F32) for ref in parts)


def body(queries, keys, values, out_grad, block_ids, block_mask):
    unit, width = queries.shape
    ctx_size, lanes = lax.axis_size("ctx"), lax.axis_size("fsdp")
    units = ctx_size // SHARE
    rows = SHARE * unit
    sub = width // GROUP
    scale = width ** (-0.5)
    factor = scale * math.log2(math.e)
    if keys.shape[1] != width:
        key_group = lax.axis_index("fsdp") // GROUP
        keys = lax.dynamic_slice_in_dim(keys, key_group * width, width, 1)
        values = lax.dynamic_slice_in_dim(values, key_group * width, width, 1)

    def swap(x, step):
        return lax.ppermute(x, "ctx", [(i, i ^ step) for i in range(ctx_size)])

    qg, kv = jnp.stack([queries, out_grad]), jnp.stack([keys, values])
    far_qg = swap(qg, 2)
    kvs = [kv] + [swap(kv, u * SHARE) for u in range(1, units)]
    limits = call(
        functools.partial(limits_kernel, units, unit // 2),
        [jax.ShapeDtypeStruct((2 * units, unit), jnp.int32)] * SHARE,
        [block_ids, block_mask],
        in_specs=[pl.BlockSpec(memory_space=pltpu.SMEM)] * 2,
    )
    (sent_qg,) = call(after_kernel, [jax.ShapeDtypeStruct(far_qg.shape, BF16)], [far_qg, limits[0]])
    qgs = [qg, swap(qg, 1), far_qg, swap(sent_qg, 1)]

    product = 2 * unit * unit * width
    grid = jax.ShapeDtypeStruct((unit, unit), F32)
    rows_out = jax.ShapeDtypeStruct((3, unit), F32)
    results = {}

    def run_tiles(tiles):
        outs = call(
            functools.partial(tile_kernel, tiles, factor),
            [grid] * (2 * len(tiles)) + [rows_out] * len(tiles),
            [limits[r] for r, _ in tiles] + [qgs[r] for r, _ in tiles] + [kvs[u] for _, u in tiles],
            flops=2 * product * len(tiles),
        )
        for i, tile in enumerate(tiles):
            results[tile] = outs[i :: len(tiles)]

    run_tiles([(0, 0), (2, 0)])
    run_tiles([(r, u) for u in range(1, units) for r in (0, 2)] + [(1, u) for u in range(units)])
    run_tiles([(3, u) for u in range(units)])
    (stats,) = call(
        functools.partial(collect_kernel, units),
        [jax.ShapeDtypeStruct((SHARE, 3, unit), F32)],
        [results[r, u][2] for r in range(SHARE) for u in range(units)],
    )
    came = {step: swap(stats, step) for step in (3, 2, 1)}
    both_stats = [stats] + [came[step] for step in range(1, SHARE)]

    parts = (GROUP, 2, sub, unit)
    scores, shares = [], []
    for u in reversed(range(units)):
        dscores, share = call(
            functools.partial(grads_kernel, scale),
            [
                jax.ShapeDtypeStruct((unit, rows), BF16),
                jax.ShapeDtypeStruct(parts, BF16 if u else F32),
            ],
            both_stats + qgs + [results[r, u][i] for i in range(3) for r in range(SHARE)],
            flops=2 * SHARE * product,
        )
        scores.insert(0, dscores)
        shares.insert(0, swap(share, u * SHARE) if u else share)
    own, *far = call(
        functools.partial(query_kernel, units, scale),
        [jax.ShapeDtypeStruct((unit, width), F32)]
        + [jax.ShapeDtypeStruct((unit, width), BF16)] * (SHARE - 1),
        scores + kvs,
        flops=SHARE * units * product,
    )
    far = [swap(x, step + 1) for step, x in enumerate(far)]

    def cross(x, step):
        pairs = [
            (c * lanes + i, c * lanes + i // GROUP * GROUP + TARGETS[c % 2][step - 1][i % GROUP])
            for c in range(ctx_size)
            for i in range(lanes)
        ]
        return lax.ppermute(x, ("ctx", "fsdp"), pairs)

    own_part, *others_part = call(
        merge_kernel,
        [jax.ShapeDtypeStruct(parts[1:], F32)]
        + [jax.ShapeDtypeStruct(parts[1:], BF16)] * (GROUP - 1),
        shares,
        scratch=[pltpu.VMEM(parts, F32)],
    )
    columns = [own_part] + [cross(others_part[h - 1], h) for h in range(1, GROUP)]
    (dq,) = call(sum_kernel, [jax.ShapeDtypeStruct((unit, width), F32)], [own] + far)
    dk, dv = call(final_kernel, [jax.ShapeDtypeStruct((sub, unit), F32)] * 2, columns)
    return dq, dk.T, dv.T


def solution(mesh):
    in_specs = (P("ctx", "fsdp"), P("ctx", None), P("ctx", None), P("ctx", "fsdp"), P(), P())
    out_specs = (P("ctx", "fsdp"), P("ctx", "fsdp"), P("ctx", "fsdp"))
    return jax.shard_map(body, mesh=mesh, in_specs=in_specs, out_specs=out_specs, check_vma=False)
```

```python
import functools
import math

import jax
import jax.numpy as jnp
from jax import lax
from jax.experimental import pallas as pl
from jax.experimental.pallas import tpu as pltpu
from jax.sharding import PartitionSpec as P

GROUP = 4
SHARE = 4
MASKED = -1e30
FLOOR = -1e20
VMEM_LIMIT = 48 * 1024 * 1024

F32 = jnp.float32
BF16 = jnp.bfloat16


def dot(left, right, left_dim, right_dim):
    return lax.dot_general(
        left, right, (((left_dim,), (right_dim,)), ((), ())), preferred_element_type=F32
    )


def vmem():
    return pl.BlockSpec(memory_space=pltpu.VMEM)


def call(kernel, out_shape, ins, in_specs=None, flops=0, scratch=()):
    size = sum(math.prod(x.shape) * x.dtype.itemsize for x in list(ins) + list(out_shape))
    return pl.pallas_call(
        kernel,
        out_shape=out_shape,
        in_specs=in_specs or [vmem() for _ in ins],
        out_specs=[vmem() for _ in out_shape],
        scratch_shapes=list(scratch),
        compiler_params=pltpu.CompilerParams(vmem_limit_bytes=VMEM_LIMIT),
        cost_estimate=pl.CostEstimate(flops=flops, bytes_accessed=size, transcendentals=0),
    )(*ins)


def limits_kernel(units, half, ids_ref, mask_ref, *limit_refs):
    ctx_index = lax.axis_index("ctx")
    lane = lax.broadcasted_iota(jnp.int32, (1, half), 1)
    for r, limit_ref in enumerate(limit_refs):
        for side in range(2):
            query_block = ids_ref[(ctx_index ^ r) * 2 + side]
            for row in range(2 * units):
                key_block = ids_ref[(ctx_index ^ (row // 2 * SHARE)) * 2 + row % 2]
                linked = mask_ref[query_block, key_block] > 0
                start = jnp.where(linked, (query_block - key_block) * half, -2 * half)
                limit_ref[row : row + 1, side * half : (side + 1) * half] = lane + start


def after_kernel(in_ref, after_ref, out_ref):
    del after_ref
    out_ref[...] = in_ref[...]


def tile_kernel(tiles, factor, *refs):
    count = len(tiles)
    limit_refs, qg_refs, kv_refs = (refs[i * count : (i + 1) * count] for i in range(3))
    exp_refs, dprob_refs, stats_refs = (refs[i * count : (i + 1) * count] for i in range(3, 6))
    unit = qg_refs[0].shape[1]
    half = unit // 2
    row = lax.broadcasted_iota(jnp.int32, (half, 1), 0)
    for i, (_, u) in enumerate(tiles):
        products = dot(kv_refs[i][0], qg_refs[i][0], 1, 1) * factor
        scores = jnp.concatenate(
            [
                jnp.where(
                    limit_refs[i][u * 2 + part : u * 2 + part + 1, :] >= row,
                    products[part * half : (part + 1) * half],
                    MASKED,
                )
                for part in range(2)
            ],
            axis=0,
        )
        top = jnp.maximum(jnp.max(scores.reshape(-1, 8, unit), axis=0), FLOOR)
        weights = jnp.exp2(scores.reshape(-1, 8, unit) - top)
        dprobs = dot(kv_refs[i][1], qg_refs[i][1], 1, 1)
        exp_refs[i][...] = weights.reshape(unit, unit)
        dprob_refs[i][...] = dprobs
        stats_refs[i][0] = top
        stats_refs[i][1] = jnp.sum(weights, axis=0)
        stats_refs[i][2] = jnp.sum(weights * dprobs.reshape(-1, 8, unit), axis=0)


def merge_stats(left, right):
    top = jnp.maximum(left[0:1], right[0:1])
    first, second = jnp.exp2(left[0:1] - top), jnp.exp2(right[0:1] - top)
    return jnp.concatenate(
        [top, left[1:2] * first + right[1:2] * second, left[2:3] * first + right[2:3] * second],
        axis=0,
    )


def collect_kernel(units, *refs):
    for r in range(SHARE):
        parts = [refs[r * units + u] for u in range(units)]
        tops = functools.reduce(jnp.maximum, [ref[0] for ref in parts])
        top = jnp.max(tops, axis=0, keepdims=True)
        factors = [jnp.exp2(ref[0] - top) for ref in parts]
        refs[-1][r, 0:1, :] = top
        for row in (1, 2):
            total = sum(ref[row] * factor for ref, factor in zip(parts, factors))
            refs[-1][r, row : row + 1, :] = jnp.sum(total, axis=0, keepdims=True)


def last_tiles_kernel(tiles, others, factor, units, *refs):
    count = len(tiles)
    ins, refs = refs[: 3 * count], refs[3 * count :]
    other_refs, outs, collected_ref = refs[: len(others)], refs[len(others) : -1], refs[-1]
    tile_kernel(tiles, factor, *ins, *outs)
    stats = dict(zip(others, other_refs)) | dict(zip(tiles, outs[2 * count :]))
    collect_kernel(units, *[stats[r, u] for r in range(SHARE) for u in range(units)], collected_ref)


def grads_kernel(scale, *refs):
    all_refs, refs = refs[:SHARE], refs[SHARE:]
    qg_refs, refs = refs[:SHARE], refs[SHARE:]
    exp_refs, dprob_refs, stats_refs = (refs[i * SHARE : (i + 1) * SHARE] for i in range(3))
    ds_ref, out_ref = refs[3 * SHARE :]
    _, unit, width = qg_refs[0].shape
    sub = width // GROUP
    dk, dv = 0.0, 0.0
    for r in range(SHARE):
        whole = functools.reduce(merge_stats, [all_refs[s][r ^ s] for s in range(SHARE)])
        share = jnp.exp2(stats_refs[r][0] - whole[0:1]) / whole[1:2]
        delta = whole[2:3] / whole[1:2]
        probs = (exp_refs[r][...].reshape(-1, 8, unit) * share).reshape(unit, unit)
        dprobs = dprob_refs[r][...]
        dscores = (probs * (dprobs - delta)).astype(BF16)
        ds_ref[:, r * unit : (r + 1) * unit] = dscores
        dv += dot(probs.astype(BF16), qg_refs[r][1], 1, 0)
        dk += dot(dscores, qg_refs[r][0], 1, 0)
    dk_tall = (dk * scale).T.astype(out_ref.dtype)
    dv_tall = dv.T.astype(out_ref.dtype)
    for part in range(GROUP):
        out_ref[part, 0] = dk_tall[part * sub : (part + 1) * sub]
        out_ref[part, 1] = dv_tall[part * sub : (part + 1) * sub]


TARGETS = (
    ((2, 3, 1, 0), (3, 2, 0, 1), (1, 0, 3, 2)),
    ((1, 3, 0, 2), (3, 2, 1, 0), (2, 0, 3, 1)),
)


def target(core, lane, h):
    place = 0
    for side in range(2):
        for i in range(GROUP):
            here = (lane == i) & (core == side)
            place = jnp.where(here, TARGETS[side][h - 1][i], place)
    return place


def merge_kernel(*refs):
    terms, total_ref, (own_ref, *far_refs) = refs[: -GROUP - 1], refs[-1], refs[-GROUP - 1 : -1]
    total_ref[...] = sum(ref[...].astype(F32) for ref in terms)
    lane, core = lax.axis_index("fsdp") % GROUP, lax.axis_index("ctx") % 2
    own_ref[...] = total_ref[lane]
    for h in range(1, GROUP):
        far_refs[h - 1][...] = total_ref[target(core, lane, h)].astype(BF16)


def query_kernel(units, scale, *refs):
    ds_refs, kv_refs = refs[:units], refs[units : 2 * units]
    own_ref, far_refs = refs[2 * units], refs[2 * units + 1 :]
    unit = own_ref.shape[0]
    dq = sum(dot(kv_refs[u][0], ds_refs[u][...], 0, 0) for u in range(units))
    dq = (dq * scale).T
    own_ref[...] = dq[:unit]
    for r in range(1, SHARE):
        far_refs[r - 1][...] = dq[r * unit : (r + 1) * unit].astype(BF16)


def sum_kernel(*refs):
    refs[-1][...] = sum(ref[...].astype(F32) for ref in refs[:-1])


def final_kernel(*refs):
    parts, (dk_ref, dv_ref) = refs[:-2], refs[-2:]
    dk_ref[...] = sum(ref[0].astype(F32) for ref in parts)
    dv_ref[...] = sum(ref[1].astype(F32) for ref in parts)


def body(queries, keys, values, out_grad, block_ids, block_mask):
    unit, width = queries.shape
    ctx_size, lanes = lax.axis_size("ctx"), lax.axis_size("fsdp")
    units = ctx_size // SHARE
    rows = SHARE * unit
    sub = width // GROUP
    scale = width ** (-0.5)
    factor = scale * math.log2(math.e)
    if keys.shape[1] != width:
        key_group = lax.axis_index("fsdp") // GROUP
        keys = lax.dynamic_slice_in_dim(keys, key_group * width, width, 1)
        values = lax.dynamic_slice_in_dim(values, key_group * width, width, 1)

    def swap(x, step):
        return lax.ppermute(x, "ctx", [(i, i ^ step) for i in range(ctx_size)])

    qg, kv = jnp.stack([queries, out_grad]), jnp.stack([keys, values])
    far_qg = swap(qg, 2)
    kvs = [kv] + [swap(kv, u * SHARE) for u in range(1, units)]
    limits = call(
        functools.partial(limits_kernel, units, unit // 2),
        [jax.ShapeDtypeStruct((2 * units, unit), jnp.int32)] * SHARE,
        [block_ids, block_mask],
        in_specs=[pl.BlockSpec(memory_space=pltpu.SMEM)] * 2,
    )
    (sent_qg,) = call(after_kernel, [jax.ShapeDtypeStruct(far_qg.shape, BF16)], [far_qg, limits[0]])
    qgs = [qg, swap(qg, 1), far_qg, swap(sent_qg, 1)]

    product = 2 * unit * unit * width
    grid = jax.ShapeDtypeStruct((unit, unit), F32)
    rows_out = jax.ShapeDtypeStruct((3, 8, unit), F32)
    results = {}

    def run_tiles(tiles):
        outs = call(
            functools.partial(tile_kernel, tiles, factor),
            [grid] * (2 * len(tiles)) + [rows_out] * len(tiles),
            [limits[r] for r, _ in tiles] + [qgs[r] for r, _ in tiles] + [kvs[u] for _, u in tiles],
            flops=2 * product * len(tiles),
        )
        for i, tile in enumerate(tiles):
            results[tile] = outs[i :: len(tiles)]

    run_tiles([(0, 0), (2, 0)])
    run_tiles([(r, u) for u in range(1, units) for r in (0, 2)] + [(1, u) for u in range(units)])
    last, others = [(3, u) for u in range(units)], list(results)
    *outs, stats = call(
        functools.partial(last_tiles_kernel, last, others, factor, units),
        [grid] * (2 * len(last))
        + [rows_out] * len(last)
        + [jax.ShapeDtypeStruct((SHARE, 3, unit), F32)],
        [limits[r] for r, _ in last]
        + [qgs[r] for r, _ in last]
        + [kvs[u] for _, u in last]
        + [results[tile][2] for tile in others],
        flops=2 * product * len(last),
    )
    for i, tile in enumerate(last):
        results[tile] = outs[i :: len(last)]
    came = {step: swap(stats, step) for step in (3, 2, 1)}
    both_stats = [stats] + [came[step] for step in range(1, SHARE)]

    parts = (GROUP, 2, sub, unit)
    scores, shares = [], []
    for u in reversed(range(units)):
        dscores, share = call(
            functools.partial(grads_kernel, scale),
            [
                jax.ShapeDtypeStruct((unit, rows), BF16),
                jax.ShapeDtypeStruct(parts, BF16 if u else F32),
            ],
            both_stats + qgs + [results[r, u][i] for i in range(3) for r in range(SHARE)],
            flops=2 * SHARE * product,
        )
        scores.insert(0, dscores)
        shares.insert(0, swap(share, u * SHARE) if u else share)
    own, *far = call(
        functools.partial(query_kernel, units, scale),
        [jax.ShapeDtypeStruct((unit, width), F32)]
        + [jax.ShapeDtypeStruct((unit, width), BF16)] * (SHARE - 1),
        scores + kvs,
        flops=SHARE * units * product,
    )
    far = [swap(x, step + 1) for step, x in enumerate(far)]

    def cross(x, step):
        pairs = [
            (c * lanes + i, c * lanes + i // GROUP * GROUP + TARGETS[c % 2][step - 1][i % GROUP])
            for c in range(ctx_size)
            for i in range(lanes)
        ]
        return lax.ppermute(x, ("ctx", "fsdp"), pairs)

    own_part, *others_part = call(
        merge_kernel,
        [jax.ShapeDtypeStruct(parts[1:], F32)]
        + [jax.ShapeDtypeStruct(parts[1:], BF16)] * (GROUP - 1),
        shares,
        scratch=[pltpu.VMEM(parts, F32)],
    )
    columns = [own_part] + [cross(others_part[h - 1], h) for h in range(1, GROUP)]
    (dq,) = call(sum_kernel, [jax.ShapeDtypeStruct((unit, width), F32)], [own] + far)
    dk, dv = call(final_kernel, [jax.ShapeDtypeStruct((sub, unit), F32)] * 2, columns)
    return dq, dk.T, dv.T


def solution(mesh):
    in_specs = (P("ctx", "fsdp"), P("ctx", None), P("ctx", None), P("ctx", "fsdp"), P(), P())
    out_specs = (P("ctx", "fsdp"), P("ctx", "fsdp"), P("ctx", "fsdp"))
    return jax.shard_map(body, mesh=mesh, in_specs=in_specs, out_specs=out_specs, check_vma=False)
```

```python
import functools
import math

import jax
import jax.numpy as jnp
from jax import lax
from jax.experimental import pallas as pl
from jax.experimental.pallas import tpu as pltpu
from jax.sharding import PartitionSpec as P

GROUP = 4
SHARE = 4
MASKED = -1e30
FLOOR = -1e20
VMEM_LIMIT = 48 * 1024 * 1024

F32 = jnp.float32
BF16 = jnp.bfloat16


def dot(left, right, left_dim, right_dim):
    return lax.dot_general(
        left, right, (((left_dim,), (right_dim,)), ((), ())), preferred_element_type=F32
    )


def vmem():
    return pl.BlockSpec(memory_space=pltpu.VMEM)


def call(kernel, out_shape, ins, in_specs=None, flops=0, scratch=()):
    size = sum(math.prod(x.shape) * x.dtype.itemsize for x in list(ins) + list(out_shape))
    return pl.pallas_call(
        kernel,
        out_shape=out_shape,
        in_specs=in_specs or [vmem() for _ in ins],
        out_specs=[vmem() for _ in out_shape],
        scratch_shapes=list(scratch),
        compiler_params=pltpu.CompilerParams(vmem_limit_bytes=VMEM_LIMIT),
        cost_estimate=pl.CostEstimate(flops=flops, bytes_accessed=size, transcendentals=0),
    )(*ins)


def limits_kernel(units, half, ids_ref, mask_ref, *limit_refs):
    ctx_index = lax.axis_index("ctx")
    lane = lax.broadcasted_iota(jnp.int32, (1, half), 1)
    for r, limit_ref in enumerate(limit_refs):
        for side in range(2):
            query_block = ids_ref[(ctx_index ^ r) * 2 + side]
            for row in range(2 * units):
                key_block = ids_ref[(ctx_index ^ (row // 2 * SHARE)) * 2 + row % 2]
                linked = mask_ref[query_block, key_block] > 0
                start = jnp.where(linked, (query_block - key_block) * half, -2 * half)
                limit_ref[row : row + 1, side * half : (side + 1) * half] = lane + start


def after_kernel(in_ref, after_ref, out_ref):
    del after_ref
    out_ref[...] = in_ref[...]


def tile_kernel(tiles, factor, *refs):
    count = len(tiles)
    limit_refs, qg_refs, kv_refs = (refs[i * count : (i + 1) * count] for i in range(3))
    exp_refs, dprob_refs, stats_refs = (refs[i * count : (i + 1) * count] for i in range(3, 6))
    unit = qg_refs[0].shape[1]
    half = unit // 2
    row = lax.broadcasted_iota(jnp.int32, (half, 1), 0)
    for i, (_, u) in enumerate(tiles):
        products = dot(kv_refs[i][0], qg_refs[i][0], 1, 1) * factor
        scores = jnp.concatenate(
            [
                jnp.where(
                    limit_refs[i][u * 2 + part : u * 2 + part + 1, :] >= row,
                    products[part * half : (part + 1) * half],
                    MASKED,
                )
                for part in range(2)
            ],
            axis=0,
        )
        top = jnp.maximum(jnp.max(scores.reshape(-1, 8, unit), axis=0), FLOOR)
        weights = jnp.exp2(scores.reshape(-1, 8, unit) - top)
        dprobs = dot(kv_refs[i][1], qg_refs[i][1], 1, 1)
        exp_refs[i][...] = weights.reshape(unit, unit)
        dprob_refs[i][...] = dprobs
        stats_refs[i][0] = top
        stats_refs[i][1] = jnp.sum(weights, axis=0)
        stats_refs[i][2] = jnp.sum(weights * dprobs.reshape(-1, 8, unit), axis=0)


def collect_kernel(units, *refs):
    for r in range(SHARE):
        parts = [refs[r * units + u] for u in range(units)]
        tops = functools.reduce(jnp.maximum, [ref[0] for ref in parts])
        top = jnp.max(tops, axis=0, keepdims=True)
        factors = [jnp.exp2(ref[0] - top) for ref in parts]
        refs[-1][r, 0:1, :] = top
        for row in (1, 2):
            total = sum(ref[row] * factor for ref, factor in zip(parts, factors))
            refs[-1][r, row : row + 1, :] = jnp.sum(total, axis=0, keepdims=True)


def last_tiles_kernel(tiles, others, factor, units, *refs):
    count = len(tiles)
    ins, refs = refs[: 3 * count], refs[3 * count :]
    other_refs, outs, collected_ref = refs[: len(others)], refs[len(others) : -1], refs[-1]
    tile_kernel(tiles, factor, *ins, *outs)
    stats = dict(zip(others, other_refs)) | dict(zip(tiles, outs[2 * count :]))
    collect_kernel(units, *[stats[r, u] for r in range(SHARE) for u in range(units)], collected_ref)


def grads_kernel(scale, *refs):
    all_refs, refs = refs[:SHARE], refs[SHARE:]
    qg_refs, refs = refs[:SHARE], refs[SHARE:]
    exp_refs, dprob_refs, stats_refs = (refs[i * SHARE : (i + 1) * SHARE] for i in range(3))
    ds_ref, out_ref = refs[3 * SHARE :]
    _, unit, width = qg_refs[0].shape
    sub = width // GROUP
    dk, dv = 0.0, 0.0
    for r in range(SHARE):
        stats = [all_refs[s][r ^ s] for s in range(SHARE)]
        top = functools.reduce(jnp.maximum, [x[0:1] for x in stats])
        factors = [jnp.exp2(x[0:1] - top) for x in stats]
        inverse = 1.0 / sum(x[1:2] * factor for x, factor in zip(stats, factors))
        share = jnp.exp2(stats_refs[r][0] - top) * inverse
        delta = sum(x[2:3] * factor for x, factor in zip(stats, factors)) * inverse
        probs = (exp_refs[r][...].reshape(-1, 8, unit) * share).reshape(unit, unit)
        dprobs = dprob_refs[r][...]
        dscores = (probs * (dprobs - delta)).astype(BF16)
        ds_ref[:, r * unit : (r + 1) * unit] = dscores
        dv += dot(probs.astype(BF16), qg_refs[r][1], 1, 0)
        dk += dot(dscores, qg_refs[r][0], 1, 0)
    dk_tall = (dk * scale).T.astype(out_ref.dtype)
    dv_tall = dv.T.astype(out_ref.dtype)
    for part in range(GROUP):
        out_ref[part, 0] = dk_tall[part * sub : (part + 1) * sub]
        out_ref[part, 1] = dv_tall[part * sub : (part + 1) * sub]


TARGETS = (
    ((2, 3, 1, 0), (3, 2, 0, 1), (1, 0, 3, 2)),
    ((1, 3, 0, 2), (3, 2, 1, 0), (2, 0, 3, 1)),
)


def target(core, lane, h):
    place = 0
    for side in range(2):
        for i in range(GROUP):
            here = (lane == i) & (core == side)
            place = jnp.where(here, TARGETS[side][h - 1][i], place)
    return place


def merge_kernel(*refs):
    terms, total_ref, (own_ref, *far_refs) = refs[: -GROUP - 1], refs[-1], refs[-GROUP - 1 : -1]
    total_ref[...] = sum(ref[...].astype(F32) for ref in terms)
    lane, core = lax.axis_index("fsdp") % GROUP, lax.axis_index("ctx") % 2
    own_ref[...] = total_ref[lane]
    for h in range(1, GROUP):
        far_refs[h - 1][...] = total_ref[target(core, lane, h)].astype(BF16)


def query_kernel(units, scale, *refs):
    ds_refs, kv_refs = refs[:units], refs[units : 2 * units]
    own_ref, far_refs = refs[2 * units], refs[2 * units + 1 :]
    unit = own_ref.shape[0]
    dq = sum(dot(kv_refs[u][0], ds_refs[u][...], 0, 0) for u in range(units))
    dq = (dq * scale).T
    own_ref[...] = dq[:unit]
    for r in range(1, SHARE):
        far_refs[r - 1][...] = dq[r * unit : (r + 1) * unit].astype(BF16)


def sum_kernel(*refs):
    refs[-1][...] = sum(ref[...].astype(F32) for ref in refs[:-1])


def final_kernel(*refs):
    parts, (dk_ref, dv_ref) = refs[:-2], refs[-2:]
    dk_ref[...] = sum(ref[0].astype(F32) for ref in parts)
    dv_ref[...] = sum(ref[1].astype(F32) for ref in parts)


def body(queries, keys, values, out_grad, block_ids, block_mask):
    unit, width = queries.shape
    ctx_size, lanes = lax.axis_size("ctx"), lax.axis_size("fsdp")
    units = ctx_size // SHARE
    rows = SHARE * unit
    sub = width // GROUP
    scale = width ** (-0.5)
    factor = scale * math.log2(math.e)
    if keys.shape[1] != width:
        key_group = lax.axis_index("fsdp") // GROUP
        keys = lax.dynamic_slice_in_dim(keys, key_group * width, width, 1)
        values = lax.dynamic_slice_in_dim(values, key_group * width, width, 1)

    def swap(x, step):
        return lax.ppermute(x, "ctx", [(i, i ^ step) for i in range(ctx_size)])

    qg, kv = jnp.stack([queries, out_grad]), jnp.stack([keys, values])
    far_qg = swap(qg, 2)
    kvs = [kv] + [swap(kv, u * SHARE) for u in range(1, units)]
    limits = call(
        functools.partial(limits_kernel, units, unit // 2),
        [jax.ShapeDtypeStruct((2 * units, unit), jnp.int32)] * SHARE,
        [block_ids, block_mask],
        in_specs=[pl.BlockSpec(memory_space=pltpu.SMEM)] * 2,
    )
    (sent_qg,) = call(after_kernel, [jax.ShapeDtypeStruct(far_qg.shape, BF16)], [far_qg, limits[0]])
    qgs = [qg, swap(qg, 1), far_qg, swap(sent_qg, 1)]

    product = 2 * unit * unit * width
    grid = jax.ShapeDtypeStruct((unit, unit), F32)
    rows_out = jax.ShapeDtypeStruct((3, 8, unit), F32)
    results = {}

    def run_tiles(tiles):
        outs = call(
            functools.partial(tile_kernel, tiles, factor),
            [grid] * (2 * len(tiles)) + [rows_out] * len(tiles),
            [limits[r] for r, _ in tiles] + [qgs[r] for r, _ in tiles] + [kvs[u] for _, u in tiles],
            flops=2 * product * len(tiles),
        )
        for i, tile in enumerate(tiles):
            results[tile] = outs[i :: len(tiles)]

    run_tiles([(0, 0), (2, 0)])
    run_tiles([(r, u) for u in range(1, units) for r in (0, 2)] + [(1, u) for u in range(units)])
    last, others = [(3, u) for u in range(units)], list(results)
    *outs, stats = call(
        functools.partial(last_tiles_kernel, last, others, factor, units),
        [grid] * (2 * len(last))
        + [rows_out] * len(last)
        + [jax.ShapeDtypeStruct((SHARE, 3, unit), F32)],
        [limits[r] for r, _ in last]
        + [qgs[r] for r, _ in last]
        + [kvs[u] for _, u in last]
        + [results[tile][2] for tile in others],
        flops=2 * product * len(last),
    )
    for i, tile in enumerate(last):
        results[tile] = outs[i :: len(last)]
    came = {step: swap(stats, step) for step in (3, 2, 1)}
    both_stats = [stats] + [came[step] for step in range(1, SHARE)]

    parts = (GROUP, 2, sub, unit)
    scores, shares = [], []
    for u in reversed(range(units)):
        dscores, share = call(
            functools.partial(grads_kernel, scale),
            [
                jax.ShapeDtypeStruct((unit, rows), BF16),
                jax.ShapeDtypeStruct(parts, BF16 if u else F32),
            ],
            both_stats + qgs + [results[r, u][i] for i in range(3) for r in range(SHARE)],
            flops=2 * SHARE * product,
        )
        scores.insert(0, dscores)
        shares.insert(0, swap(share, u * SHARE) if u else share)
    own, *far = call(
        functools.partial(query_kernel, units, scale),
        [jax.ShapeDtypeStruct((unit, width), F32)]
        + [jax.ShapeDtypeStruct((unit, width), BF16)] * (SHARE - 1),
        scores + kvs,
        flops=SHARE * units * product,
    )
    far = [swap(x, step + 1) for step, x in enumerate(far)]

    def cross(x, step):
        pairs = [
            (c * lanes + i, c * lanes + i // GROUP * GROUP + TARGETS[c % 2][step - 1][i % GROUP])
            for c in range(ctx_size)
            for i in range(lanes)
        ]
        return lax.ppermute(x, ("ctx", "fsdp"), pairs)

    own_part, *others_part = call(
        merge_kernel,
        [jax.ShapeDtypeStruct(parts[1:], F32)]
        + [jax.ShapeDtypeStruct(parts[1:], BF16)] * (GROUP - 1),
        shares,
        scratch=[pltpu.VMEM(parts, F32)],
    )
    columns = [own_part] + [cross(others_part[h - 1], h) for h in range(1, GROUP)]
    (dq,) = call(sum_kernel, [jax.ShapeDtypeStruct((unit, width), F32)], [own] + far)
    dk, dv = call(final_kernel, [jax.ShapeDtypeStruct((sub, unit), F32)] * 2, columns)
    return dq, dk.T, dv.T


def solution(mesh):
    in_specs = (P("ctx", "fsdp"), P("ctx", None), P("ctx", None), P("ctx", "fsdp"), P(), P())
    out_specs = (P("ctx", "fsdp"), P("ctx", "fsdp"), P("ctx", "fsdp"))
    return jax.shard_map(body, mesh=mesh, in_specs=in_specs, out_specs=out_specs, check_vma=False)
```

```python
import functools
import math

import jax
import jax.numpy as jnp
from jax import lax
from jax.experimental import pallas as pl
from jax.experimental.pallas import tpu as pltpu
from jax.sharding import PartitionSpec as P

GROUP = 4
SHARE = 4
MASKED = -1e30
FLOOR = -1e20
VMEM_LIMIT = 48 * 1024 * 1024

F32 = jnp.float32
BF16 = jnp.bfloat16


def dot(left, right, left_dim, right_dim):
    return lax.dot_general(
        left, right, (((left_dim,), (right_dim,)), ((), ())), preferred_element_type=F32
    )


def vmem():
    return pl.BlockSpec(memory_space=pltpu.VMEM)


def call(kernel, out_shape, ins, in_specs=None, flops=0, scratch=()):
    size = sum(math.prod(x.shape) * x.dtype.itemsize for x in list(ins) + list(out_shape))
    return pl.pallas_call(
        kernel,
        out_shape=out_shape,
        in_specs=in_specs or [vmem() for _ in ins],
        out_specs=[vmem() for _ in out_shape],
        scratch_shapes=list(scratch),
        compiler_params=pltpu.CompilerParams(vmem_limit_bytes=VMEM_LIMIT),
        cost_estimate=pl.CostEstimate(flops=flops, bytes_accessed=size, transcendentals=0),
    )(*ins)


def limits_kernel(units, half, ids_ref, mask_ref, *limit_refs):
    ctx_index = lax.axis_index("ctx")
    lane = lax.broadcasted_iota(jnp.int32, (1, half), 1)
    for r, limit_ref in enumerate(limit_refs):
        for side in range(2):
            query_block = ids_ref[(ctx_index ^ r) * 2 + side]
            for row in range(2 * units):
                key_block = ids_ref[(ctx_index ^ (row // 2 * SHARE)) * 2 + row % 2]
                linked = mask_ref[query_block, key_block] > 0
                start = jnp.where(linked, (query_block - key_block) * half, -2 * half)
                limit_ref[row : row + 1, side * half : (side + 1) * half] = lane + start


def after_kernel(in_ref, after_ref, out_ref):
    del after_ref
    out_ref[...] = in_ref[...]


def tile_kernel(tiles, factor, *refs):
    count = len(tiles)
    limit_refs, qg_refs, kv_refs = (refs[i * count : (i + 1) * count] for i in range(3))
    exp_refs, dprob_refs, stats_refs = (refs[i * count : (i + 1) * count] for i in range(3, 6))
    unit = qg_refs[0].shape[1]
    half = unit // 2
    row = lax.broadcasted_iota(jnp.int32, (half, 1), 0)
    for i, (_, u) in enumerate(tiles):
        products = dot(kv_refs[i][0], qg_refs[i][0], 1, 1) * factor
        scores = jnp.concatenate(
            [
                jnp.where(
                    limit_refs[i][u * 2 + part : u * 2 + part + 1, :] >= row,
                    products[part * half : (part + 1) * half],
                    MASKED,
                )
                for part in range(2)
            ],
            axis=0,
        )
        top = jnp.maximum(jnp.max(scores.reshape(-1, 8, unit), axis=0), FLOOR)
        weights = jnp.exp2(scores.reshape(-1, 8, unit) - top)
        dprobs = dot(kv_refs[i][1], qg_refs[i][1], 1, 1)
        exp_refs[i][...] = weights.reshape(unit, unit)
        dprob_refs[i][...] = dprobs
        stats_refs[i][0] = top
        stats_refs[i][1] = jnp.sum(weights, axis=0)
        stats_refs[i][2] = jnp.sum(weights * dprobs.reshape(-1, 8, unit), axis=0)


def collect_kernel(units, *refs):
    for r in range(SHARE):
        parts = [refs[r * units + u] for u in range(units)]
        tops = functools.reduce(jnp.maximum, [ref[0] for ref in parts])
        top = jnp.max(tops, axis=0, keepdims=True)
        factors = [jnp.exp2(ref[0] - top) for ref in parts]
        refs[-1][r, 0:1, :] = top
        for row in (1, 2):
            total = sum(ref[row] * factor for ref, factor in zip(parts, factors))
            refs[-1][r, row : row + 1, :] = jnp.sum(total, axis=0, keepdims=True)


def last_tiles_kernel(tiles, others, factor, units, *refs):
    count = len(tiles)
    ins, refs = refs[: 3 * count], refs[3 * count :]
    other_refs, outs, collected_ref = refs[: len(others)], refs[len(others) : -1], refs[-1]
    tile_kernel(tiles, factor, *ins, *outs)
    stats = dict(zip(others, other_refs)) | dict(zip(tiles, outs[2 * count :]))
    collect_kernel(units, *[stats[r, u] for r in range(SHARE) for u in range(units)], collected_ref)


def grads_kernel(scale, *refs):
    all_refs, refs = refs[:SHARE], refs[SHARE:]
    qg_refs, refs = refs[:SHARE], refs[SHARE:]
    exp_refs, dprob_refs, stats_refs = (refs[i * SHARE : (i + 1) * SHARE] for i in range(3))
    ds_ref, out_ref = refs[3 * SHARE :]
    _, unit, width = qg_refs[0].shape
    sub = width // GROUP
    dk, dv = 0.0, 0.0
    for r in range(SHARE):
        stats = [all_refs[s][r ^ s] for s in range(SHARE)]
        top = functools.reduce(jnp.maximum, [x[0:1] for x in stats])
        factors = [jnp.exp2(x[0:1] - top) for x in stats]
        inverse = 1.0 / sum(x[1:2] * factor for x, factor in zip(stats, factors))
        share = jnp.exp2(stats_refs[r][0] - top) * inverse
        delta = sum(x[2:3] * factor for x, factor in zip(stats, factors)) * inverse
        probs = (exp_refs[r][...].reshape(-1, 8, unit) * share).reshape(unit, unit)
        dprobs = dprob_refs[r][...]
        dscores = (probs * (dprobs - delta)).astype(BF16)
        ds_ref[:, r * unit : (r + 1) * unit] = dscores
        dv += dot(probs.astype(BF16), qg_refs[r][1], 1, 0)
        dk += dot(dscores, qg_refs[r][0], 1, 0)
    dk_tall = (dk * scale).T.astype(out_ref.dtype)
    dv_tall = dv.T.astype(out_ref.dtype)
    for part in range(GROUP):
        out_ref[part, 0] = dk_tall[part * sub : (part + 1) * sub]
        out_ref[part, 1] = dv_tall[part * sub : (part + 1) * sub]


TARGETS = (
    ((2, 3, 1, 0), (3, 2, 0, 1), (1, 0, 3, 2)),
    ((1, 2, 3, 0), (2, 3, 0, 1), (3, 0, 1, 2)),
)


def target(core, lane, h):
    place = 0
    for side in range(2):
        for i in range(GROUP):
            here = (lane == i) & (core == side)
            place = jnp.where(here, TARGETS[side][h - 1][i], place)
    return place


def merge_kernel(*refs):
    terms, total_ref, (own_ref, *far_refs) = refs[: -GROUP - 1], refs[-1], refs[-GROUP - 1 : -1]
    total_ref[...] = sum(ref[...].astype(F32) for ref in terms)
    lane, core = lax.axis_index("fsdp") % GROUP, lax.axis_index("ctx") % 2
    own_ref[...] = total_ref[lane]
    for h in range(1, GROUP):
        far_refs[h - 1][...] = total_ref[target(core, lane, h)].astype(BF16)


def query_kernel(units, scale, *refs):
    ds_refs, kv_refs = refs[:units], refs[units : 2 * units]
    own_ref, far_refs = refs[2 * units], refs[2 * units + 1 :]
    unit = own_ref.shape[0]
    dq = sum(dot(kv_refs[u][0], ds_refs[u][...], 0, 0) for u in range(units))
    dq = (dq * scale).T
    own_ref[...] = dq[:unit]
    for r in range(1, SHARE):
        far_refs[r - 1][...] = dq[r * unit : (r + 1) * unit].astype(BF16)


def sum_kernel(*refs):
    refs[-1][...] = sum(ref[...].astype(F32) for ref in refs[:-1])


def final_kernel(*refs):
    parts, (dk_ref, dv_ref) = refs[:-2], refs[-2:]
    dk_ref[...] = sum(ref[0].astype(F32) for ref in parts)
    dv_ref[...] = sum(ref[1].astype(F32) for ref in parts)


def body(queries, keys, values, out_grad, block_ids, block_mask):
    unit, width = queries.shape
    ctx_size, lanes = lax.axis_size("ctx"), lax.axis_size("fsdp")
    units = ctx_size // SHARE
    rows = SHARE * unit
    sub = width // GROUP
    scale = width ** (-0.5)
    factor = scale * math.log2(math.e)
    if keys.shape[1] != width:
        key_group = lax.axis_index("fsdp") // GROUP
        keys = lax.dynamic_slice_in_dim(keys, key_group * width, width, 1)
        values = lax.dynamic_slice_in_dim(values, key_group * width, width, 1)

    def swap(x, step):
        return lax.ppermute(x, "ctx", [(i, i ^ step) for i in range(ctx_size)])

    qg, kv = jnp.stack([queries, out_grad]), jnp.stack([keys, values])
    far_qg = swap(qg, 2)
    kvs = [kv] + [swap(kv, u * SHARE) for u in range(1, units)]
    limits = call(
        functools.partial(limits_kernel, units, unit // 2),
        [jax.ShapeDtypeStruct((2 * units, unit), jnp.int32)] * SHARE,
        [block_ids, block_mask],
        in_specs=[pl.BlockSpec(memory_space=pltpu.SMEM)] * 2,
    )
    (sent_qg,) = call(after_kernel, [jax.ShapeDtypeStruct(far_qg.shape, BF16)], [far_qg, limits[0]])
    qgs = [qg, swap(qg, 1), far_qg, swap(sent_qg, 1)]

    product = 2 * unit * unit * width
    grid = jax.ShapeDtypeStruct((unit, unit), F32)
    rows_out = jax.ShapeDtypeStruct((3, 8, unit), F32)
    results = {}

    def run_tiles(tiles):
        outs = call(
            functools.partial(tile_kernel, tiles, factor),
            [grid] * (2 * len(tiles)) + [rows_out] * len(tiles),
            [limits[r] for r, _ in tiles] + [qgs[r] for r, _ in tiles] + [kvs[u] for _, u in tiles],
            flops=2 * product * len(tiles),
        )
        for i, tile in enumerate(tiles):
            results[tile] = outs[i :: len(tiles)]

    run_tiles([(0, 0), (2, 0)])
    run_tiles([(r, u) for u in range(1, units) for r in (0, 2)] + [(1, u) for u in range(units)])
    last, others = [(3, u) for u in range(units)], list(results)
    *outs, stats = call(
        functools.partial(last_tiles_kernel, last, others, factor, units),
        [grid] * (2 * len(last))
        + [rows_out] * len(last)
        + [jax.ShapeDtypeStruct((SHARE, 3, unit), F32)],
        [limits[r] for r, _ in last]
        + [qgs[r] for r, _ in last]
        + [kvs[u] for _, u in last]
        + [results[tile][2] for tile in others],
        flops=2 * product * len(last),
    )
    for i, tile in enumerate(last):
        results[tile] = outs[i :: len(last)]
    came = {step: swap(stats, step) for step in (3, 2, 1)}
    both_stats = [stats] + [came[step] for step in range(1, SHARE)]

    parts = (GROUP, 2, sub, unit)
    scores, shares = [], []
    for u in reversed(range(units)):
        dscores, share = call(
            functools.partial(grads_kernel, scale),
            [
                jax.ShapeDtypeStruct((unit, rows), BF16),
                jax.ShapeDtypeStruct(parts, BF16 if u else F32),
            ],
            both_stats + qgs + [results[r, u][i] for i in range(3) for r in range(SHARE)],
            flops=2 * SHARE * product,
        )
        scores.insert(0, dscores)
        shares.insert(0, swap(share, u * SHARE) if u else share)
    own, *far = call(
        functools.partial(query_kernel, units, scale),
        [jax.ShapeDtypeStruct((unit, width), F32)]
        + [jax.ShapeDtypeStruct((unit, width), BF16)] * (SHARE - 1),
        scores + kvs,
        flops=SHARE * units * product,
    )
    far = [swap(x, step + 1) for step, x in enumerate(far)]

    def cross(x, step):
        pairs = [
            (c * lanes + i, c * lanes + i // GROUP * GROUP + TARGETS[c % 2][step - 1][i % GROUP])
            for c in range(ctx_size)
            for i in range(lanes)
        ]
        return lax.ppermute(x, ("ctx", "fsdp"), pairs)

    own_part, *others_part = call(
        merge_kernel,
        [jax.ShapeDtypeStruct(parts[1:], F32)]
        + [jax.ShapeDtypeStruct(parts[1:], BF16)] * (GROUP - 1),
        shares,
        scratch=[pltpu.VMEM(parts, F32)],
    )
    columns = [own_part] + [cross(others_part[h - 1], h) for h in range(1, GROUP)]
    (dq,) = call(sum_kernel, [jax.ShapeDtypeStruct((unit, width), F32)], [own] + far)
    dk, dv = call(final_kernel, [jax.ShapeDtypeStruct((sub, unit), F32)] * 2, columns)
    return dq, dk.T, dv.T


def solution(mesh):
    in_specs = (P("ctx", "fsdp"), P("ctx", None), P("ctx", None), P("ctx", "fsdp"), P(), P())
    out_specs = (P("ctx", "fsdp"), P("ctx", "fsdp"), P("ctx", "fsdp"))
    return jax.shard_map(body, mesh=mesh, in_specs=in_specs, out_specs=out_specs, check_vma=False)
```
